128 devices in a mesh: curve: 8 (over x, core), tile: 16 (over z, y).
Axes of the slice: x: 4, y: 4, z: 4, core: 2. Of those that a mesh axis runs over, the one named last changes fastest.
Arguments:
- points: bfloat16 [65536, 512], P(('curve', 'tile')), may hold values from -16 to 16
- neighbours: int32 [27, 65536], P(None, ('curve', 'tile')), may hold values from 448 to 1536, as said below
- conv_weight: bfloat16 [27, 512, 512], replicated, may hold values from -0.078125 to 0.078125
- cpe_gain: float32 [512], replicated, may hold values from 0.1 to 1.9
- w_query: bfloat16 [512, 512], replicated, may hold values from -2 to 2
- w_key: bfloat16 [512, 512], replicated, may hold values from -20 to 20
- w_value: bfloat16 [512, 512], replicated, may hold values from -0.25 to 0.25
- w_out: bfloat16 [512, 512], replicated, may hold values from -0.25 to 0.25
- w_up: bfloat16 [512, 2048], replicated, may hold values from -0.25 to 0.25
- w_down: bfloat16 [2048, 512], replicated, may hold values from -0.125 to 0.125
- w_pool: bfloat16 [512, 512], replicated, may hold values from -0.25 to 0.25
- pool_gain: float32 [512], replicated, may hold values from 0.1 to 1.9
- send_slot: int32 [65536], P(('curve', 'tile')), may hold values from 0 to 1023, as said below
- arrival_from: int32 [131072], P(('curve', 'tile')), may hold values from 0 to 1024, as said below
- pool_pick: int32 [128, 128], P(('curve', 'tile')), may hold values from 0 to 127, each once within a row
- cell_from: int32 [128, 128], P(('curve', 'tile')), may hold values from 0 to 127, each once within a row
Outputs:
- fine_out: bfloat16 [131072, 512], P(('curve', 'tile'))
- pooled: bfloat16 [16384, 512], P(('curve', 'tile'))
The draws below stay inside these ranges and needn't reach their ends.
Inputs may be any that keep to these rules, and one draw needn't show every extreme that they name: neighbours[13, r] = 512 + r % 512, the point itself; the value 3 * 512 marks a missing neighbour; every other value v satisfies |v - 512 - r % 512| <= 64, so that it lies in 448 .. 1087, and both ends of that range occur in every draw. `send_slot`: the 512 values of one device's points are distinct, so one device sends at most 8 points to one owner; in every draw some owner receives exactly 8 points from every device. `arrival_from`: the 1024 values of one owner name every incoming index that some point has there exactly once, and 1024 in every other slot; in every draw some owner has all its slots filled. `pool_pick`: each owner's row is a permutation of 0 .. 127. `cell_from`: each coarse owner's row is a permutation of 0 .. 127.
All inputs are finite; a program needn't handle non-finite values.
Results may differ from the reference program's by a relative error of at most 0.012.
Values may be sent and summed in bfloat16 or wider, within the bound.
A program may use at most 128 MiB of HBM per device.

```python
import math
import jax
import jax.numpy as jnp
from jax import lax

C = 512
HEADS = 32
HID = 2048
CAP = 1024
KERNEL = 27
POOL = 8
RIM = 64
OWNERS = 128
OWN = 1024
P_DEV = 512
ROWS = 65536
SLOT = 8
WIN = 128
WPP = 1
CELLS = 16384
SLOTS_ALL = 131072


def draw_points(key, part):
    root_key = jax.random.fold_in(key, 3)
    return jnp.clip(jax.random.normal(root_key, (ROWS, C), jnp.float32), -6.0, 6.0).astype(jnp.bfloat16)


def draw_neighbours(key, part):
    root_key = jax.random.fold_in(key, 17)
    key_pick, key_keep = jax.random.split(root_key, 2)
    position = jnp.arange(ROWS, dtype=jnp.int32) % P_DEV
    reach = jax.random.randint(key_pick, (KERNEL, ROWS), -RIM, RIM)
    picks = P_DEV + position[None, :] + reach
    keeping = jax.random.randint(key_keep, (KERNEL, ROWS), 0, 2)
    chosen_rows = jnp.where(keeping == 1, picks, 3 * P_DEV)
    centre = P_DEV + position
    chosen_rows = chosen_rows.at[(KERNEL - 1) // 2].set(centre)
    chosen_rows = chosen_rows.at[0, 0].set(P_DEV - RIM)
    chosen_rows = chosen_rows.at[KERNEL - 1, P_DEV - 1].set(2 * P_DEV + RIM - 1)
    return chosen_rows.astype(jnp.int32)


def query_key_pair(key):
    root_key = jax.random.fold_in(key, 11)
    base_part = jnp.clip(jax.random.normal(jax.random.fold_in(root_key, 1), (C, C), jnp.float32), -6.0, 6.0) / math.sqrt(C)
    other_part = jnp.clip(jax.random.normal(jax.random.fold_in(root_key, 2), (C, C), jnp.float32), -6.0, 6.0) / math.sqrt(C)
    return (base_part, other_part)


def draw_w_query(key, part):
    base_part, other_part = query_key_pair(key)
    return base_part.astype(jnp.bfloat16)


def draw_w_key(key, part):
    base_part, other_part = query_key_pair(key)
    return other_part.astype(jnp.bfloat16)


def route_tables(key):
    root_key = jax.random.fold_in(key, 5)
    key_level, key_full, key_jitter, key_shuffle, key_place = jax.random.split(root_key, 5)
    total_slots = OWNERS * SLOT
    levels = jax.random.randint(key_level, (OWNERS,), 0, 4)
    fullest = jax.random.randint(key_full, (), 0, OWNERS)
    targets = jnp.arange(total_slots, dtype=jnp.int32) // SLOT
    jitter = jax.random.randint(key_jitter, (OWNERS, total_slots), 0, 256)
    scores = levels[targets][None, :] * 64 + jitter
    scores = jnp.where((targets == fullest)[None, :], 1000000, scores)
    ranking = jnp.argsort(-scores, axis=1, stable=True)
    picked = ranking[:, :P_DEV]
    shuffles = jax.vmap(lambda sub_key: jax.random.permutation(sub_key, P_DEV))(jax.random.split(key_shuffle, OWNERS))
    send_slots = jnp.take_along_axis(picked, shuffles, axis=1).reshape(ROWS)
    sources = jnp.arange(OWNERS, dtype=jnp.int32)[:, None]
    filled = jnp.zeros((OWNERS, total_slots), jnp.int32).at[sources, picked].set(1)
    incoming = filled.reshape(OWNERS, OWNERS, SLOT).transpose(1, 0, 2).reshape(OWNERS, total_slots)
    placing = jax.vmap(lambda sub_key: jax.random.permutation(sub_key, total_slots))(jax.random.split(key_place, OWNERS))
    markers = jnp.where(incoming == 1, jnp.arange(total_slots, dtype=jnp.int32)[None, :], total_slots)
    arrivals = jnp.full((OWNERS, total_slots), total_slots, jnp.int32).at[sources, placing].set(markers)
    return (send_slots.astype(jnp.int32), arrivals.reshape(OWNERS * total_slots).astype(jnp.int32))


def draw_send_slot(key, part):
    send_slots, arrivals = route_tables(key)
    return send_slots


def draw_arrival_from(key, part):
    send_slots, arrivals = route_tables(key)
    return arrivals


def bell_draw(stream_key, dims, deviation, limit, held_as=jnp.bfloat16):
    return jnp.clip(deviation * jax.random.normal(stream_key, dims, jnp.float32), -limit, limit).astype(held_as)


def setup_inputs(seed: int = 0) -> dict:
    key_list = jax.random.split(jax.random.key(seed), 17)
    return {
        "points": draw_points(jax.random.fold_in(key_list[16], 71), 0),
        "neighbours": draw_neighbours(jax.random.fold_in(key_list[16], 71), 0),
        "conv_weight": bell_draw(key_list[2], (KERNEL, C, C), (KERNEL * C // 2) ** -0.5, 0.078125),
        "cpe_gain": jnp.clip(1.0 + 0.18 * jax.random.normal(key_list[3], (C,), jnp.float32), 0.1, 1.9),
        "w_query": draw_w_query(jax.random.fold_in(key_list[16], 71), 0),
        "w_key": draw_w_key(jax.random.fold_in(key_list[16], 71), 0),
        "w_value": bell_draw(key_list[6], (C, C), C ** -0.5, 0.25),
        "w_out": bell_draw(key_list[7], (C, C), C ** -0.5, 0.25),
        "w_up": bell_draw(key_list[8], (C, HID), C ** -0.5, 0.25),
        "w_down": bell_draw(key_list[9], (HID, C), HID ** -0.5, 0.125),
        "w_pool": bell_draw(key_list[10], (C, C), C ** -0.5, 0.25),
        "pool_gain": jnp.clip(1.0 + 0.18 * jax.random.normal(key_list[11], (C,), jnp.float32), 0.1, 1.9),
        "send_slot": draw_send_slot(jax.random.fold_in(key_list[16], 71), 0),
        "arrival_from": draw_arrival_from(jax.random.fold_in(key_list[16], 71), 0),
        "pool_pick": jax.vmap(lambda own: jax.random.permutation(own, WIN))(jax.random.split(key_list[14], OWNERS)).reshape((OWNERS, WIN)).astype(jnp.int32),
        "cell_from": jax.vmap(lambda own: jax.random.permutation(own, WIN))(jax.random.split(key_list[15], OWNERS)).reshape((OWNERS, WIN)).astype(jnp.int32),
    }


def layer_norm(values):
    centre = lax.optimization_barrier(jnp.mean(values, axis=-1, keepdims=True))
    spread = lax.optimization_barrier(jnp.mean((values - centre) ** 2, axis=-1, keepdims=True))
    return (values - centre) * lax.rsqrt(spread + 1e-05)

def patch_attention(query, keys, values, live):
    slots, width = query.shape
    head_dim = width // HEADS
    per_group = min(HEADS, 4)
    groups = HEADS // per_group
    span = per_group * head_dim
    scale = 1.0 / math.sqrt(head_dim)

    def attend(counter):
        patch = counter // groups
        column = counter % groups * span
        start = patch * CAP
        q_block = lax.dynamic_slice(query, (start, column), (CAP, span)).reshape(CAP, per_group, head_dim)
        k_block = lax.dynamic_slice(keys, (start, column), (CAP, span)).reshape(CAP, per_group, head_dim)
        v_block = lax.dynamic_slice(values, (start, column), (CAP, span)).reshape(CAP, per_group, head_dim)
        allowed = lax.dynamic_slice_in_dim(live, start, CAP)
        scores = jnp.einsum('qhd,khd->hqk', q_block.astype(jnp.float32), k_block.astype(jnp.float32), preferred_element_type=jnp.float32) * scale
        scores = jnp.where(allowed[None, None, :], scores, -1e+30)
        shifted = jnp.exp(scores - lax.optimization_barrier(jnp.max(scores, axis=-1, keepdims=True)))
        probs = (shifted / lax.optimization_barrier(jnp.sum(shifted, axis=-1, keepdims=True))).astype(jnp.bfloat16)
        result = jnp.einsum('hqk,khd->qhd', probs.astype(jnp.float32), v_block.astype(jnp.float32), preferred_element_type=jnp.float32)
        return result.astype(jnp.bfloat16).reshape(CAP, span)
    counters = jnp.arange(slots // CAP * groups, dtype=jnp.int32)
    blocks = lax.map(attend, counters)
    return blocks.reshape(slots // CAP, groups, CAP, span).transpose(0, 2, 1, 3).reshape(slots, width)

def owner_block(arranged, live, w_query, w_key, w_value, w_out, w_up, w_down, w_pool):
    normed = layer_norm(arranged.astype(jnp.float32)).astype(jnp.bfloat16)
    query = jnp.dot(normed, w_query, preferred_element_type=jnp.float32).astype(jnp.bfloat16)
    keys = jnp.dot(normed, w_key, preferred_element_type=jnp.float32).astype(jnp.bfloat16)
    values = jnp.dot(normed, w_value, preferred_element_type=jnp.float32).astype(jnp.bfloat16)
    attended = patch_attention(query, keys, values, live)
    mixed = arranged.astype(jnp.float32) + jnp.dot(attended, w_out, preferred_element_type=jnp.float32)
    second = layer_norm(mixed).astype(jnp.bfloat16)
    inner = jax.nn.gelu(jnp.dot(second, w_up, preferred_element_type=jnp.float32), approximate=False).astype(jnp.bfloat16)
    fine = mixed + jnp.dot(inner, w_down, preferred_element_type=jnp.float32)
    fine = jnp.where(live[:, None], fine, 0.0).astype(jnp.bfloat16)
    pool_rows = jnp.dot(fine, w_pool, preferred_element_type=jnp.float32)
    sums = lax.optimization_barrier(jnp.sum(pool_rows.reshape(OWN // POOL, POOL, C), axis=1))
    counts = lax.optimization_barrier(jnp.sum(live.reshape(OWN // POOL, POOL).astype(jnp.float32), axis=1))
    means = (sums / jnp.maximum(counts, 1.0)[:, None]).astype(jnp.bfloat16)
    return (fine, means)

def reference(points, neighbours, conv_weight, cpe_gain, w_query, w_key, w_value, w_out, w_up, w_down, w_pool, pool_gain, send_slot, arrival_from, pool_pick, cell_from):
    block_start = jnp.arange(ROWS, dtype=jnp.int32) // P_DEV * P_DEV
    padded = jnp.concatenate([jnp.zeros((P_DEV, C), jnp.bfloat16), points, jnp.zeros((P_DEV + 1, C), jnp.bfloat16)], axis=0)
    targets = jnp.where(neighbours < 3 * P_DEV, block_start[None, :] + neighbours, ROWS + 2 * P_DEV).astype(jnp.int32)

    def conv_step(running, carried):
        index_row, weight_slab = carried
        picked = jnp.take(padded, index_row, axis=0)
        return (running + jnp.dot(picked, weight_slab, preferred_element_type=jnp.float32), None)
    conv, _ = lax.scan(conv_step, jnp.zeros((ROWS, C), jnp.float32), (targets, conv_weight))
    lifted = (points.astype(jnp.float32) + cpe_gain * layer_norm(conv)).astype(jnp.bfloat16)
    source = jnp.arange(ROWS, dtype=jnp.int32) // P_DEV
    owner = send_slot // SLOT
    incoming = source * SLOT + send_slot % SLOT
    sectioning = jnp.zeros((OWNERS * OWN + 1, C), jnp.bfloat16).at[(owner * OWN + incoming).astype(jnp.int32)].set(lifted)
    slot_owner = jnp.arange(SLOTS_ALL, dtype=jnp.int32) // OWN
    pick_rows = jnp.where(arrival_from < OWN, slot_owner * OWN + arrival_from, OWNERS * OWN).astype(jnp.int32)
    arranged = jnp.take(sectioning, pick_rows, axis=0).reshape(OWNERS, OWN, C)
    live = (arrival_from < OWN).reshape(OWNERS, OWN)

    def per_owner(carried):
        return owner_block(carried[0], carried[1], w_query, w_key, w_value, w_out, w_up, w_down, w_pool)
    fine, means = lax.map(per_owner, (arranged, live))
    outgoing = jnp.take_along_axis(means, pool_pick[:, :, None].astype(jnp.int32), axis=1)
    position = jnp.arange(WIN, dtype=jnp.int32)
    coarse = jnp.broadcast_to((position // WPP)[None, :], (OWNERS, WIN)).astype(jnp.int32)
    arrive_index = (jnp.arange(OWNERS, dtype=jnp.int32)[:, None] * WPP + (position % WPP)[None, :]).astype(jnp.int32)
    arrived = jnp.zeros((OWNERS, WIN, C), jnp.bfloat16).at[coarse, arrive_index].set(outgoing)
    gathered = jnp.take_along_axis(arrived, cell_from[:, :, None].astype(jnp.int32), axis=1)
    pooled = jax.nn.gelu(pool_gain * layer_norm(gathered.astype(jnp.float32)), approximate=False).astype(jnp.bfloat16)
    return (fine.reshape(SLOTS_ALL, C), pooled.reshape(CELLS, C))
```

```python
import functools
import math

import jax
import jax.numpy as jnp
from jax import lax
from jax.experimental import pallas as pl
from jax.experimental.pallas import tpu as pltpu
from jax.sharding import PartitionSpec as P

F32 = jnp.float32
BF16 = jnp.bfloat16
I32 = jnp.int32

C = 512
HEADS = 32
HEAD = C // HEADS
HID = 2048
KERNEL = 27
OWNERS = 128
OWN = 1024
ROWS = 512
RIM = 64
WIN = 128
BLOCK = 128
GROUP = 3
CHUNKS = KERNEL // GROUP
LANES = 128
GROUPS = C // LANES
PER_GROUP = LANES // HEAD
Q_BLOCK = 512
SCALE = math.log2(math.e) / math.sqrt(HEAD)

VMEM_LIMIT = 60 * 1024 * 1024


def dot(a, b):
    return jnp.dot(a, b, preferred_element_type=F32)


def norm_rows(v):
    centre = jnp.mean(v, axis=-1, keepdims=True)
    shifted = v - centre
    spread = jnp.mean(shifted * shifted, axis=-1, keepdims=True)
    return shifted * lax.rsqrt(spread + 1e-05)


def conv_kernel(window_ref, rel_ref, slot_ref, gain_ref, weight_hbm, out_ref, weight, picked, total, sems):
    copies = [
        pltpu.make_async_copy(
            weight_hbm.at[pl.ds(c * GROUP * C, GROUP * C)],
            weight.at[pl.ds(c * GROUP * C, GROUP * C)],
            sems.at[c],
        )
        for c in range(CHUNKS)
    ]
    for copy in copies:
        copy.start()
    lane = lax.broadcasted_iota(I32, (BLOCK, 2 * BLOCK), 1)
    for c in range(CHUNKS):
        for j in range(GROUP):
            k = c * GROUP + j
            for b in range(ROWS // BLOCK):
                rows = pl.ds(b * BLOCK, BLOCK)
                hot = (rel_ref[rows, k : k + 1] == lane).astype(F32).astype(BF16)
                near = window_ref[pl.ds(b * BLOCK, 2 * BLOCK), :]
                picked[rows, pl.ds(j * C, C)] = dot(hot, near).astype(BF16)
        copies[c].wait()
        part = dot(picked[...], weight[pl.ds(c * GROUP * C, GROUP * C), :])
        if c == 0:
            total[...] = part
        else:
            total[...] += part
    own = window_ref[pl.ds(RIM, ROWS), :].astype(F32)
    lifted = (own + gain_ref[...] * norm_rows(total[...])).astype(BF16)
    slot = lax.broadcasted_iota(I32, (OWN, ROWS), 0)
    hot = (slot == slot_ref[...]).astype(F32).astype(BF16)
    moved = dot(hot, lifted).reshape(OWNERS, 8, C)
    out_ref[...] = jnp.concatenate([moved[:, :, : C // 2], moved[:, :, C // 2 :]], axis=1).astype(BF16)


def conv_call(window, rel, slot, gain, weight):
    vmem = pl.BlockSpec(memory_space=pltpu.VMEM)
    return pl.pallas_call(
        conv_kernel,
        out_shape=jax.ShapeDtypeStruct((OWNERS, 16, C // 2), BF16),
        in_specs=[vmem, vmem, vmem, vmem, pl.BlockSpec(memory_space=pl.ANY)],
        out_specs=vmem,
        scratch_shapes=[
            pltpu.VMEM((KERNEL * C, C), BF16),
            pltpu.VMEM((ROWS, GROUP * C), BF16),
            pltpu.VMEM((ROWS, C), F32),
            pltpu.SemaphoreType.DMA((CHUNKS,)),
        ],
        compiler_params=pltpu.CompilerParams(vmem_limit_bytes=VMEM_LIMIT),
        cost_estimate=pl.CostEstimate(flops=11_000_000_000, bytes_accessed=16_000_000, transcendentals=0),
    )(window, rel, slot, gain, weight)


def owner_kernel(
    arrived_ref, from_row_ref, from_col_ref, pick_ref, wq_hbm, wk_hbm, wv_hbm, wo_hbm, wu_hbm, wd_hbm, wp_hbm,
    fine_ref, sending_ref,
    wq, wk, wv, wo, wu, wd, wp, arranged, query, keys, values, attended, mixed, sems,
):
    pairs = [(wq_hbm, wq), (wk_hbm, wk), (wv_hbm, wv), (wo_hbm, wo), (wu_hbm, wu), (wd_hbm, wd), (wp_hbm, wp)]
    copies = [pltpu.make_async_copy(src, dst, sems.at[i]) for i, (src, dst) in enumerate(pairs)]
    for copy in copies:
        copy.start()
    got = arrived_ref[...].astype(F32)
    got = jnp.concatenate([got[:, :8, :], got[:, 8:, :]], axis=2).astype(BF16).reshape(OWN, C)
    source = lax.broadcasted_iota(I32, (OWN, OWN), 1)
    hot = (from_col_ref[...] == source).astype(F32).astype(BF16)
    placed = dot(hot, got)
    arranged[...] = placed
    normed = norm_rows(placed).astype(BF16)
    live_col = from_col_ref[...] < OWN
    place = lax.broadcasted_iota(I32, (8, OWN), 1)
    first = jnp.min(jnp.where(from_row_ref[...] < OWN, place, OWN), axis=1, keepdims=True)
    stand_in = dot((place == first).astype(F32).astype(BF16), normed)[0:1, :]
    normed_keys = jnp.where(live_col, normed.astype(F32), stand_in).astype(BF16)
    copies[0].wait()
    query[...] = (dot(normed, wq[...]) * SCALE).astype(BF16)
    copies[1].wait()
    keys[...] = dot(normed_keys, wk[...]).astype(BF16)
    copies[2].wait()
    values[...] = dot(normed, wv[...]).astype(BF16)

    lane = lax.broadcasted_iota(I32, (1, LANES), 1)
    live = jnp.broadcast_to(live_col.astype(F32), (OWN, LANES)).astype(BF16)

    @pl.loop(0, GROUPS)
    def _(g):
        columns = pl.ds(pl.multiple_of(g * LANES, LANES), LANES)
        k_group = keys[:, columns]
        v_group = values[:, columns]

        @pl.loop(0, OWN // Q_BLOCK)
        def _(b):
            rows = pl.ds(pl.multiple_of(b * Q_BLOCK, Q_BLOCK), Q_BLOCK)
            q_block = query[rows, columns]
            total = jnp.zeros((Q_BLOCK, 2 * LANES), F32)
            for h in range(PER_GROUP):
                mine = ((lane >= h * HEAD) & (lane < (h + 1) * HEAD)).astype(F32).astype(BF16)
                k_head = k_group * mine
                v_head = jnp.concatenate([v_group * mine, live * mine], axis=1)
                scores = lax.dot_general(q_block, k_head, (((1,), (1,)), ((), ())), preferred_element_type=F32)
                top = jnp.max(scores, axis=1, keepdims=True)
                probs = jnp.exp2((scores - top).astype(BF16))
                total = total + dot(probs, v_head)
            attended[rows, columns] = (total[:, :LANES] / total[:, LANES:]).astype(BF16)

    copies[3].wait()
    mixed[...] = arranged[...] + dot(attended[...], wo[...])
    copies[4].wait()
    copies[5].wait()

    @pl.loop(0, OWN // 256)
    def _(b):
        rows = pl.ds(pl.multiple_of(b * 256, 256), 256)
        mix = mixed[rows, :]
        second = norm_rows(mix).astype(BF16)
        up = dot(second, wu[...])
        inner = (0.5 * up * (1.0 + lax.erf(up * (1.0 / math.sqrt(2.0))))).astype(BF16)
        fine = mix + dot(inner, wd[...])
        fine_ref[rows, :] = jnp.where(from_col_ref[rows, :] < OWN, fine, 0.0).astype(BF16)

    slot = lax.broadcasted_iota(I32, (WIN, OWN), 1) // 8
    cell = lax.broadcasted_iota(I32, (WIN, OWN), 0)
    member = (slot == cell).astype(F32).astype(BF16)
    sums = dot(member, fine_ref[...])
    counts = dot(member, live)[:, 0:1]
    high = sums.astype(BF16)
    low = (sums - high.astype(F32)).astype(BF16)
    copies[6].wait()
    means = ((dot(high, wp[...]) + dot(low, wp[...])) / jnp.maximum(counts, 1.0)).astype(BF16)
    cells = lax.broadcasted_iota(I32, (WIN, WIN), 1)
    sending_ref[...] = dot((pick_ref[...] == cells).astype(F32).astype(BF16), means).astype(BF16)


def owner_call(arrived, from_row, from_col, pick, *weights):
    vmem = pl.BlockSpec(memory_space=pltpu.VMEM)
    hbm = pl.BlockSpec(memory_space=pl.ANY)
    return pl.pallas_call(
        owner_kernel,
        out_shape=(jax.ShapeDtypeStruct((OWN, C), BF16), jax.ShapeDtypeStruct((WIN, C), BF16)),
        in_specs=[vmem] * 4 + [hbm] * 7,
        out_specs=(vmem, vmem),
        scratch_shapes=[
            pltpu.VMEM((C, C), BF16),
            pltpu.VMEM((C, C), BF16),
            pltpu.VMEM((C, C), BF16),
            pltpu.VMEM((C, C), BF16),
            pltpu.VMEM((C, HID), BF16),
            pltpu.VMEM((HID, C), BF16),
            pltpu.VMEM((C, C), BF16),
            pltpu.VMEM((OWN, C), F32),
            pltpu.VMEM((OWN, C), BF16),
            pltpu.VMEM((OWN, C), BF16),
            pltpu.VMEM((OWN, C), BF16),
            pltpu.VMEM((OWN, C), BF16),
            pltpu.VMEM((OWN, C), F32),
            pltpu.SemaphoreType.DMA((7,)),
        ],
        compiler_params=pltpu.CompilerParams(vmem_limit_bytes=VMEM_LIMIT),
        cost_estimate=pl.CostEstimate(flops=40_000_000_000, bytes_accessed=10_000_000, transcendentals=40_000_000),
    )(arrived, from_row, from_col, pick, *weights)


def coarse_kernel(landed_ref, from_ref, gain_ref, out_ref):
    source = lax.broadcasted_iota(I32, (WIN, WIN), 1)
    gathered = dot((from_ref[...] == source).astype(F32).astype(BF16), landed_ref[...])
    value = gain_ref[...] * norm_rows(gathered)
    out_ref[...] = (0.5 * value * (1.0 + lax.erf(value * (1.0 / math.sqrt(2.0))))).astype(BF16)


def coarse_call(landed, cell_from, gain):
    vmem = pl.BlockSpec(memory_space=pltpu.VMEM)
    return pl.pallas_call(
        coarse_kernel,
        out_shape=jax.ShapeDtypeStruct((WIN, C), BF16),
        in_specs=[vmem] * 3,
        out_specs=vmem,
    )(landed, cell_from, gain)


AXES = ("curve", "tile")


def shards(
    points, neighbours, conv_weight, cpe_gain, w_query, w_key, w_value, w_out, w_up, w_down, w_pool, pool_gain,
    send_slot, arrival_from, pool_pick, cell_from,
):
    count = lax.axis_size(AXES)
    before = lax.ppermute(points[ROWS - RIM :], AXES, [(i, i + 1) for i in range(count - 1)])
    after = lax.ppermute(points[:RIM], AXES, [(i + 1, i) for i in range(count - 1)])
    window = jnp.concatenate([before, points, after], axis=0)
    base = ROWS - RIM + BLOCK * (jnp.arange(ROWS, dtype=I32) // BLOCK)
    rel = (neighbours - base[None, :]).T
    outgoing = conv_call(
        window, rel, send_slot[None, :], cpe_gain[None, :], conv_weight.reshape(KERNEL * C, C)
    )
    arrived = lax.all_to_all(outgoing, AXES, split_axis=0, concat_axis=0, tiled=True)
    fine_out, sending = owner_call(
        arrived, arrival_from[None, :], arrival_from[:, None], pool_pick.reshape(WIN, 1),
        w_query, w_key, w_value, w_out, w_up, w_down, w_pool,
    )
    landed = lax.all_to_all(sending, AXES, split_axis=0, concat_axis=0, tiled=True)
    pooled = coarse_call(landed, cell_from.reshape(WIN, 1), pool_gain[None, :])
    return fine_out, pooled


def solution(mesh):
    split = P(AXES)
    rows = P(AXES, None)
    in_specs = (rows, P(None, AXES)) + (P(),) * 10 + (split, split, rows, rows)
    return jax.shard_map(shards, mesh=mesh, in_specs=in_specs, out_specs=(rows, rows), check_vma=False)
```

```python
import math

import jax
import jax.numpy as jnp
from jax import lax
from jax.experimental import pallas as pl
from jax.experimental.pallas import tpu as pltpu
from jax.sharding import PartitionSpec as P

F32 = jnp.float32
BF16 = jnp.bfloat16
I32 = jnp.int32

C = 512
HEADS = 32
HEAD = C // HEADS
HID = 2048
KERNEL = 27
OWNERS = 128
OWN = 1024
ROWS = 512
RIM = 64
WIN = 128
BLOCK = 128
CHUNKS = 9
SPAN = KERNEL * C // CHUNKS
CURVE = 8
TILE = 16
MESH = pl.DeviceIdType.MESH
LANES = 128
GROUPS = C // LANES
PER_GROUP = LANES // HEAD
Q_BLOCK = 512
SCALE = math.log2(math.e) / math.sqrt(HEAD)

VMEM_LIMIT = 60 * 1024 * 1024


def dot(a, b):
    return jnp.dot(a, b, preferred_element_type=F32)


def norm_rows(v):
    centre = jnp.mean(v, axis=-1, keepdims=True)
    shifted = v - centre
    spread = jnp.mean(shifted * shifted, axis=-1, keepdims=True)
    return shifted * lax.rsqrt(spread + 1e-05)


def hot(columns, wanted):
    return (columns == wanted).astype(F32).astype(BF16)


def place_of():
    return lax.axis_index("curve"), lax.axis_index("tile")


def greet(curve, tile):
    barrier = pltpu.get_barrier_semaphore()

    @pl.loop(1, CURVE)
    def _(s):
        pl.semaphore_signal(barrier, inc=1, device_id=(lax.rem(curve + s, CURVE), tile), device_id_type=MESH)

    @pl.loop(1, TILE)
    def _(s):
        pl.semaphore_signal(barrier, inc=1, device_id=(curve, lax.rem(tile + s, TILE)), device_id_type=MESH)

    return barrier


def send(src, dst, sems, i, device):
    pltpu.make_async_remote_copy(
        src_ref=src, dst_ref=dst, send_sem=sems.at[i], recv_sem=sems.at[i + 1], device_id=device, device_id_type=MESH
    ).start()


def drain(ref, sem):
    pltpu.make_async_copy(ref, ref, sem).wait()


class AlongCurve:
    def __init__(self, src, dst, sems, i, curve, tile):
        self.args = src, dst, sems, i, curve, tile

    def start(self):
        src, dst, sems, i, curve, tile = self.args

        @pl.loop(1, CURVE)
        def _(s):
            peer = lax.rem(curve + s, CURVE)
            send(src.at[peer], dst.at[curve], sems, i, (peer, tile))

    def wait_recv(self):
        _, dst, sems, i, _, _ = self.args
        drain(dst.at[pl.ds(0, CURVE - 1)], sems.at[i + 1])

    def wait_send(self):
        src, _, sems, i, _, _ = self.args
        drain(src.at[pl.ds(0, CURVE - 1)], sems.at[i])

    def own(self, sem):
        src, dst, _, _, curve, _ = self.args
        return pltpu.make_async_copy(src.at[curve], dst.at[curve], sem)


class AlongTile:
    def __init__(self, src, dst, sems, i, curve, tile):
        self.args = src, dst, sems, i, curve, tile

    def start(self):
        src, dst, sems, i, curve, tile = self.args

        @pl.loop(1, TILE)
        def _(s):
            peer = lax.rem(tile + s, TILE)
            send(src.at[:, peer], dst.at[:, tile], sems, i, (curve, peer))

    def wait_recv(self):
        _, dst, sems, i, _, _ = self.args
        drain(dst.at[:, pl.ds(0, TILE - 1)], sems.at[i + 1])

    def wait_send(self):
        src, _, sems, i, _, _ = self.args
        drain(src.at[:, pl.ds(0, TILE - 1)], sems.at[i])

    def own(self, sem):
        src, dst, _, _, _, tile = self.args
        return pltpu.make_async_copy(src.at[:, tile], dst.at[:, tile], sem)


def conv_kernel(
    points_ref, near_ref, slot_ref, gain_ref, weight_hbm, left_out, right_out,
    weight, picked, window, total, left_src, right_src, left_mid, right_mid, weight_sems, sems,
):
    curve, tile = place_of()
    me = curve * TILE + tile
    after = lax.rem(me + 1, OWNERS)
    before = lax.rem(me + OWNERS - 1, OWNERS)
    copies = [
        pltpu.make_async_copy(
            weight_hbm.at[pl.ds(c * SPAN, SPAN)], weight.at[pl.ds(c * SPAN, SPAN)], weight_sems.at[c]
        )
        for c in range(CHUNKS)
    ]
    for copy in copies:
        copy.start()
    barrier = greet(curve, tile)
    for peer in (after, before):
        pl.semaphore_signal(
            barrier, inc=1, device_id=(lax.div(peer, TILE), lax.rem(peer, TILE)), device_id_type=MESH
        )
    window[pl.ds(RIM, ROWS), :] = points_ref[...]
    near = near_ref[...] - (ROWS - RIM)
    near = jnp.concatenate([near, jnp.zeros((32 - KERNEL, ROWS), I32)], axis=0).T
    lane = lax.broadcasted_iota(I32, (BLOCK, 2 * BLOCK), 1)

    def pick(b, row):
        local = near[b * BLOCK : (b + 1) * BLOCK] - b * BLOCK
        rows = window[pl.ds(b * BLOCK, 2 * BLOCK), :]
        for k in range(KERNEL):
            picked[pl.ds(row, BLOCK), pl.ds(k * C, C)] = dot(hot(local[:, k : k + 1], lane), rows).astype(BF16)

    def conv(row, count, wait):
        rows = pl.ds(row, count)
        for c in range(CHUNKS):
            if wait:
                copies[c].wait()
            part = dot(picked[rows, pl.ds(c * SPAN, SPAN)], weight[pl.ds(c * SPAN, SPAN), :])
            if c == 0:
                total[rows, :] = part
            else:
                total[rows, :] += part

    pick(1, 1 * BLOCK)
    pick(2, 2 * BLOCK)
    pl.semaphore_wait(barrier, CURVE + TILE)
    low, high = pl.ds(0, RIM), pl.ds(RIM + ROWS, RIM)
    up = pltpu.make_async_remote_copy(
        src_ref=points_ref.at[pl.ds(ROWS - RIM, RIM)], dst_ref=window.at[low], send_sem=sems.at[10],
        recv_sem=sems.at[11], device_id=(lax.div(after, TILE), lax.rem(after, TILE)), device_id_type=MESH,
    )
    down = pltpu.make_async_remote_copy(
        src_ref=points_ref.at[pl.ds(0, RIM)], dst_ref=window.at[high], send_sem=sems.at[12],
        recv_sem=sems.at[13], device_id=(lax.div(before, TILE), lax.rem(before, TILE)), device_id_type=MESH,
    )
    up.start()
    down.start()
    conv(1 * BLOCK, 2 * BLOCK, True)
    up.wait()
    down.wait()

    @pl.when(me == 0)
    def _():
        window[low, :] = jnp.zeros((RIM, C), BF16)

    @pl.when(me == OWNERS - 1)
    def _():
        window[high, :] = jnp.zeros((RIM, C), BF16)

    pick(0, 0)
    pick(3, 3 * BLOCK)
    conv(0, BLOCK, False)
    conv(3 * BLOCK, BLOCK, False)
    lifted = (points_ref[...].astype(F32) + gain_ref[...] * norm_rows(total[...])).astype(BF16)
    slots = hot(lax.broadcasted_iota(I32, (OWN, ROWS), 0), slot_ref[...])

    def outgoing(first):
        moved = dot(slots, lifted[:, first : first + C // 2]).reshape(OWNERS, 8, C // 2)
        blocks = jnp.concatenate([moved[:, :, :LANES], moved[:, :, LANES:]], axis=1).astype(BF16)
        return blocks.reshape(CURVE, TILE, 16, LANES)

    left_one = AlongCurve(left_src, left_mid, sems, 0, curve, tile)
    right_one = AlongTile(right_src, right_mid, sems, 2, curve, tile)
    left_two = AlongTile(left_mid, left_out, sems, 4, curve, tile)
    right_two = AlongCurve(right_mid, right_out, sems, 6, curve, tile)
    left_src[...] = outgoing(0)
    left_one.start()
    left_own = left_one.own(sems.at[8])
    left_own.start()
    right_src[...] = outgoing(C // 2)
    right_one.start()
    right_own = right_one.own(sems.at[9])
    right_own.start()
    left_own.wait()
    left_one.wait_recv()
    left_two.start()
    left_last = left_two.own(sems.at[8])
    left_last.start()
    right_own.wait()
    right_one.wait_recv()
    right_two.start()
    right_last = right_two.own(sems.at[9])
    right_last.start()
    left_last.wait()
    right_last.wait()
    left_two.wait_recv()
    right_two.wait_recv()
    left_one.wait_send()
    right_one.wait_send()
    left_two.wait_send()
    right_two.wait_send()


def conv_call(points, near, slot, gain, weight):
    vmem = pl.BlockSpec(memory_space=pltpu.VMEM)
    half = (CURVE, TILE, 16, LANES)
    return pl.pallas_call(
        conv_kernel,
        out_shape=(jax.ShapeDtypeStruct(half, BF16),) * 2,
        in_specs=[vmem, vmem, vmem, vmem, pl.BlockSpec(memory_space=pl.ANY)],
        out_specs=(vmem, vmem),
        scratch_shapes=[
            pltpu.VMEM((KERNEL * C, C), BF16),
            pltpu.VMEM((ROWS, KERNEL * C), BF16),
            pltpu.VMEM((ROWS + 2 * RIM, C), BF16),
            pltpu.VMEM((ROWS, C), F32),
            pltpu.VMEM(half, BF16),
            pltpu.VMEM(half, BF16),
            pltpu.VMEM(half, BF16),
            pltpu.VMEM(half, BF16),
            pltpu.SemaphoreType.DMA((CHUNKS,)),
            pltpu.SemaphoreType.DMA((14,)),
        ],
        compiler_params=pltpu.CompilerParams(vmem_limit_bytes=VMEM_LIMIT, collective_id=0, has_side_effects=True),
        cost_estimate=pl.CostEstimate(flops=12_000_000_000, bytes_accessed=18_000_000, transcendentals=0),
    )(points, near, slot, gain, weight)


def gelu(v):
    return 0.5 * v * (1.0 + lax.erf(v * (1.0 / math.sqrt(2.0))))


def owner_kernel(
    left_ref, right_ref, from_ref, pick_ref, cell_ref, gain_ref,
    wq_hbm, wk_hbm, wv_hbm, wo_hbm, wu_hbm, wd_hbm, wp_hbm,
    fine_ref, pooled_ref,
    wq, wk, wv, wo, wu, wd, wp, arranged, query, keys, values, attended, mixed,
    cell_src, cell_mid, cell_turn, cell_land, weight_sems, sems,
):
    curve, tile = place_of()
    pairs = [(wq_hbm, wq), (wk_hbm, wk), (wv_hbm, wv), (wo_hbm, wo), (wu_hbm, wu), (wd_hbm, wd), (wp_hbm, wp)]
    copies = [pltpu.make_async_copy(src, dst, weight_sems.at[i]) for i, (src, dst) in enumerate(pairs)]
    for copy in copies:
        copy.start()
    barrier = greet(curve, tile)
    tables = jnp.concatenate([from_ref[...], pick_ref[...], cell_ref[...], jnp.zeros((6, LANES), I32)], axis=0).T
    from_col = jnp.concatenate([tables[:, j : j + 1] for j in range(8)], axis=0)
    pick_col = tables[:, 8:9]
    cell_col = tables[:, 9:10]
    left = left_ref[...].reshape(OWNERS, 16, LANES).astype(F32)
    right = right_ref[...].reshape(OWNERS, 16, LANES).astype(F32)
    got = jnp.concatenate([left[:, :8], left[:, 8:], right[:, :8], right[:, 8:]], axis=2)
    got = got.astype(BF16).reshape(OWN, C)
    placed = dot(hot(from_col, lax.broadcasted_iota(I32, (OWN, OWN), 1)), got)
    arranged[...] = placed
    normed = norm_rows(placed).astype(BF16)
    live_col = from_col < OWN
    place = lax.broadcasted_iota(I32, (8, LANES), 0) * LANES + lax.broadcasted_iota(I32, (8, LANES), 1)
    first = jnp.min(jnp.where(from_ref[...] < OWN, place, OWN), axis=(0, 1), keepdims=True)
    stand_in = dot(hot(lax.broadcasted_iota(I32, (8, OWN), 1), first), normed)[0:1, :]
    normed_keys = jnp.where(live_col, normed.astype(F32), stand_in).astype(BF16)
    copies[0].wait()
    query[...] = (dot(normed, wq[...]) * SCALE).astype(BF16)
    copies[1].wait()
    keys[...] = dot(normed_keys, wk[...]).T.astype(BF16)
    copies[2].wait()
    values[...] = dot(normed, wv[...]).astype(BF16)

    lane = lax.broadcasted_iota(I32, (1, LANES), 1)
    line = lax.broadcasted_iota(I32, (LANES, 1), 0)
    live = jnp.broadcast_to(live_col.astype(F32), (OWN, LANES)).astype(BF16)

    @pl.loop(0, GROUPS)
    def _(g):
        columns = pl.ds(pl.multiple_of(g * LANES, LANES), LANES)
        k_group = keys[columns, :]
        v_group = values[:, columns]

        @pl.loop(0, OWN // Q_BLOCK)
        def _(b):
            rows = pl.ds(pl.multiple_of(b * Q_BLOCK, Q_BLOCK), Q_BLOCK)
            q_block = query[rows, columns]
            all_probs, all_values = [], []
            for h in range(PER_GROUP):
                mine = ((lane >= h * HEAD) & (lane < (h + 1) * HEAD)).astype(F32).astype(BF16)
                mine_lines = ((line >= h * HEAD) & (line < (h + 1) * HEAD)).astype(F32).astype(BF16)
                scores = dot(q_block, k_group * mine_lines)
                top = jnp.max(scores, axis=1, keepdims=True)
                all_probs.append(jnp.exp2(scores - top).astype(BF16))
                all_values.append(jnp.concatenate([v_group * mine, live * mine], axis=1))
            total = dot(jnp.concatenate(all_probs, axis=1), jnp.concatenate(all_values, axis=0))
            attended[rows, columns] = (total[:, :LANES] / total[:, LANES:]).astype(BF16)

    copies[3].wait()
    mixed[...] = arranged[...] + dot(attended[...], wo[...])
    copies[4].wait()
    copies[5].wait()
    for b in range(OWN // 256):
        rows = pl.ds(b * 256, 256)
        mix = mixed[rows, :]
        second = norm_rows(mix).astype(BF16)
        inner = gelu(dot(second, wu[...])).astype(BF16)
        fine = mix + dot(inner, wd[...])
        fine_ref[rows, :] = jnp.where(live_col[b * 256 : (b + 1) * 256], fine, 0.0).astype(BF16)

    slot = lax.broadcasted_iota(I32, (WIN, OWN), 1) // 8
    cell = lax.broadcasted_iota(I32, (WIN, OWN), 0)
    member = hot(slot, cell)
    sums = dot(member, fine_ref[...])
    counts = dot(member, live)[:, 0:1]
    high = sums.astype(BF16)
    low = (sums - high.astype(F32)).astype(BF16)
    copies[6].wait()
    means = ((dot(high, wp[...]) + dot(low, wp[...])) / jnp.maximum(counts, 1.0)).astype(BF16)
    cells = lax.broadcasted_iota(I32, (WIN, WIN), 1)
    cell_src[...] = dot(hot(pick_col, cells), means).astype(BF16).reshape(CURVE, TILE, C)
    one = AlongCurve(cell_src, cell_mid, sems, 0, curve, tile)
    pl.semaphore_wait(barrier, CURVE + TILE - 2)
    one.start()
    own = one.own(sems.at[4])
    own.start()
    own.wait()
    one.wait_recv()
    row = lax.broadcasted_iota(I32, (WIN, 1), 0)
    turned = lax.rem(row, CURVE) * TILE + lax.div(row, CURVE)
    turn = dot(hot(turned, cells), cell_mid[...].reshape(WIN, C)).reshape(TILE, CURVE, C)
    cell_turn[...] = jnp.concatenate([turn[:, :, : C // 2], turn[:, :, C // 2 :]], axis=1).astype(BF16)

    @pl.loop(1, TILE)
    def _(s):
        peer = lax.rem(tile + s, TILE)
        send(cell_turn.at[peer], cell_land.at[tile], sems, 2, (curve, peer))

    own = pltpu.make_async_copy(cell_turn.at[tile], cell_land.at[tile], sems.at[4])
    own.start()
    own.wait()
    drain(cell_land.at[pl.ds(0, TILE - 1)], sems.at[3])
    landed = cell_land[...].astype(F32)
    landed = jnp.concatenate([landed[:, :CURVE], landed[:, CURVE:]], axis=2).astype(BF16).reshape(WIN, C)
    source = lax.rem(cells, CURVE) * TILE + lax.div(cells, CURVE)
    gathered = dot(hot(cell_col, source), landed)
    pooled_ref[...] = gelu(gain_ref[...] * norm_rows(gathered)).astype(BF16)
    one.wait_send()
    drain(cell_turn.at[pl.ds(0, TILE - 1)], sems.at[2])


def owner_call(left, right, from_rows, pick, cell, gain, *weights):
    vmem = pl.BlockSpec(memory_space=pltpu.VMEM)
    hbm = pl.BlockSpec(memory_space=pl.ANY)
    return pl.pallas_call(
        owner_kernel,
        out_shape=(jax.ShapeDtypeStruct((OWN, C), BF16), jax.ShapeDtypeStruct((WIN, C), BF16)),
        in_specs=[vmem] * 6 + [hbm] * 7,
        out_specs=(vmem, vmem),
        scratch_shapes=[
            pltpu.VMEM((C, C), BF16),
            pltpu.VMEM((C, C), BF16),
            pltpu.VMEM((C, C), BF16),
            pltpu.VMEM((C, C), BF16),
            pltpu.VMEM((C, HID), BF16),
            pltpu.VMEM((HID, C), BF16),
            pltpu.VMEM((C, C), BF16),
            pltpu.VMEM((OWN, C), F32),
            pltpu.VMEM((OWN, C), BF16),
            pltpu.VMEM((C, OWN), BF16),
            pltpu.VMEM((OWN, C), BF16),
            pltpu.VMEM((OWN, C), BF16),
            pltpu.VMEM((OWN, C), F32),
            pltpu.VMEM((CURVE, TILE, C), BF16),
            pltpu.VMEM((CURVE, TILE, C), BF16),
            pltpu.VMEM((TILE, 16, C // 2), BF16),
            pltpu.VMEM((TILE, 16, C // 2), BF16),
            pltpu.SemaphoreType.DMA((7,)),
            pltpu.SemaphoreType.DMA((5,)),
        ],
        compiler_params=pltpu.CompilerParams(vmem_limit_bytes=VMEM_LIMIT, collective_id=1, has_side_effects=True),
        cost_estimate=pl.CostEstimate(flops=40_000_000_000, bytes_accessed=10_000_000, transcendentals=40_000_000),
    )(left, right, from_rows, pick, cell, gain, *weights)


AXES = ("curve", "tile")


def shards(
    points, neighbours, conv_weight, cpe_gain, w_query, w_key, w_value, w_out, w_up, w_down, w_pool, pool_gain,
    send_slot, arrival_from, pool_pick, cell_from,
):
    left, right = conv_call(
        points, neighbours, send_slot[None, :], cpe_gain[None, :], conv_weight.reshape(KERNEL * C, C)
    )
    return owner_call(
        left, right, arrival_from.reshape(8, LANES), pool_pick, cell_from, pool_gain[None, :],
        w_query, w_key, w_value, w_out, w_up, w_down, w_pool,
    )


def solution(mesh):
    split = P(AXES)
    rows = P(AXES, None)
    in_specs = (rows, P(None, AXES)) + (P(),) * 10 + (split, split, rows, rows)
    return jax.shard_map(shards, mesh=mesh, in_specs=in_specs, out_specs=(rows, rows), check_vma=False)
```

```python
import math

import jax
import jax.numpy as jnp
from jax import lax
from jax.experimental import pallas as pl
from jax.experimental.pallas import tpu as pltpu
from jax.sharding import PartitionSpec as P

F32 = jnp.float32
BF16 = jnp.bfloat16
I32 = jnp.int32
F8 = jnp.float8_e4m3fn
SUB = 64
TOP = 256.0
TINY = 1e-12

C = 512
HEADS = 32
HEAD = C // HEADS
HID = 2048
KERNEL = 27
OWNERS = 128
OWN = 1024
ROWS = 512
RIM = 64
WIN = 128
BLOCK = 128
CHUNKS = 9
SPAN = KERNEL * C // CHUNKS
CURVE = 8
TILE = 16
MESH = pl.DeviceIdType.MESH
LANES = 128
GROUPS = C // LANES
PER_GROUP = LANES // HEAD
Q_BLOCK = 1024
SCALE = math.log2(math.e) / math.sqrt(HEAD)

VMEM_LIMIT = 60 * 1024 * 1024


def dot(a, b):
    return jnp.dot(a, b, preferred_element_type=F32)


def norm_rows(v):
    centre = jnp.mean(v, axis=-1, keepdims=True)
    shifted = v - centre
    spread = jnp.mean(shifted * shifted, axis=-1, keepdims=True)
    return shifted * lax.rsqrt(spread + 1e-05)


def hot(columns, wanted):
    return (columns == wanted).astype(F32).astype(BF16)


def place_of():
    return lax.axis_index("curve"), lax.axis_index("tile")


def greet(curve, tile):
    barrier = pltpu.get_barrier_semaphore()

    @pl.loop(1, CURVE)
    def _(s):
        pl.semaphore_signal(barrier, inc=1, device_id=(lax.rem(curve + s, CURVE), tile), device_id_type=MESH)

    @pl.loop(1, TILE)
    def _(s):
        pl.semaphore_signal(barrier, inc=1, device_id=(curve, lax.rem(tile + s, TILE)), device_id_type=MESH)

    return barrier


def send(src, dst, sems, i, device):
    pltpu.make_async_remote_copy(
        src_ref=src, dst_ref=dst, send_sem=sems.at[i], recv_sem=sems.at[i + 1], device_id=device, device_id_type=MESH
    ).start()


def drain(ref, sem):
    pltpu.make_async_copy(ref, ref, sem).wait()


class AlongCurve:
    def __init__(self, src, dst, sems, i, curve, tile):
        self.args = src, dst, sems, i, curve, tile

    def start(self):
        src, dst, sems, i, curve, tile = self.args

        @pl.loop(1, CURVE)
        def _(s):
            peer = lax.rem(curve + s, CURVE)
            send(src.at[peer], dst.at[curve], sems, i, (peer, tile))

    def wait_recv(self):
        _, dst, sems, i, _, _ = self.args
        drain(dst.at[pl.ds(0, CURVE - 1)], sems.at[i + 1])

    def wait_send(self):
        src, _, sems, i, _, _ = self.args
        drain(src.at[pl.ds(0, CURVE - 1)], sems.at[i])

    def own(self, sem):
        src, dst, _, _, curve, _ = self.args
        return pltpu.make_async_copy(src.at[curve], dst.at[curve], sem)


class AlongTile:
    def __init__(self, src, dst, sems, i, curve, tile):
        self.args = src, dst, sems, i, curve, tile

    def start(self):
        src, dst, sems, i, curve, tile = self.args

        @pl.loop(1, TILE)
        def _(s):
            peer = lax.rem(tile + s, TILE)
            send(src.at[:, peer], dst.at[:, tile], sems, i, (curve, peer))

    def wait_recv(self):
        _, dst, sems, i, _, _ = self.args
        drain(dst.at[:, pl.ds(0, TILE - 1)], sems.at[i + 1])

    def wait_send(self):
        src, _, sems, i, _, _ = self.args
        drain(src.at[:, pl.ds(0, TILE - 1)], sems.at[i])

    def own(self, sem):
        src, dst, _, _, _, tile = self.args
        return pltpu.make_async_copy(src.at[:, tile], dst.at[:, tile], sem)


def conv_kernel(
    points_ref, near_ref, slot_ref, gain_ref, weight_hbm, left_out, right_out,
    weight, picked, window, total, left_src, right_src, left_mid, right_mid, weight_sems, sems,
):
    curve, tile = place_of()
    me = curve * TILE + tile
    after = lax.rem(me + 1, OWNERS)
    before = lax.rem(me + OWNERS - 1, OWNERS)
    copies = [
        pltpu.make_async_copy(
            weight_hbm.at[pl.ds(c * SPAN, SPAN)], weight.at[pl.ds(c * SPAN, SPAN)], weight_sems.at[c]
        )
        for c in range(CHUNKS)
    ]
    for copy in copies:
        copy.start()
    barrier = greet(curve, tile)
    for peer in (after, before):
        pl.semaphore_signal(
            barrier, inc=1, device_id=(lax.div(peer, TILE), lax.rem(peer, TILE)), device_id_type=MESH
        )
    window[pl.ds(RIM, ROWS), :] = points_ref[...]
    near = near_ref[...] - (ROWS - RIM)
    near = jnp.concatenate([near, jnp.zeros((32 - KERNEL, ROWS), I32)], axis=0).T
    lane = lax.broadcasted_iota(I32, (BLOCK, 2 * BLOCK), 1)

    def pick(b, row):
        local = near[b * BLOCK : (b + 1) * BLOCK] - b * BLOCK
        rows = window[pl.ds(b * BLOCK, 2 * BLOCK), :]
        for k in range(KERNEL):
            picked[pl.ds(row, BLOCK), pl.ds(k * C, C)] = dot(hot(local[:, k : k + 1], lane), rows).astype(BF16)

    def conv(row, count, wait):
        rows = pl.ds(row, count)
        for c in range(CHUNKS):
            if wait:
                copies[c].wait()
            part = dot(picked[rows, pl.ds(c * SPAN, SPAN)], weight[pl.ds(c * SPAN, SPAN), :])
            if c == 0:
                total[rows, :] = part
            else:
                total[rows, :] += part

    pick(1, 0)
    pick(2, BLOCK)
    pl.semaphore_wait(barrier, CURVE + TILE)
    low, high = pl.ds(0, RIM), pl.ds(RIM + ROWS, RIM)
    up = pltpu.make_async_remote_copy(
        src_ref=points_ref.at[pl.ds(ROWS - RIM, RIM)], dst_ref=window.at[low], send_sem=sems.at[10],
        recv_sem=sems.at[11], device_id=(lax.div(after, TILE), lax.rem(after, TILE)), device_id_type=MESH,
    )
    down = pltpu.make_async_remote_copy(
        src_ref=points_ref.at[pl.ds(0, RIM)], dst_ref=window.at[high], send_sem=sems.at[12],
        recv_sem=sems.at[13], device_id=(lax.div(before, TILE), lax.rem(before, TILE)), device_id_type=MESH,
    )
    up.start()
    down.start()
    conv(0, 2 * BLOCK, True)
    up.wait()
    down.wait()

    @pl.when(me == 0)
    def _():
        window[low, :] = jnp.zeros((RIM, C), BF16)

    @pl.when(me == OWNERS - 1)
    def _():
        window[high, :] = jnp.zeros((RIM, C), BF16)

    pick(0, 2 * BLOCK)
    pick(3, 3 * BLOCK)
    conv(2 * BLOCK, 2 * BLOCK, False)
    own = jnp.concatenate([points_ref[pl.ds(b * BLOCK, BLOCK), :] for b in (1, 2, 0, 3)], axis=0)
    lifted = (own.astype(F32) + gain_ref[...] * norm_rows(total[...])).astype(BF16)
    wanted = jnp.concatenate([slot_ref[:, b * BLOCK : (b + 1) * BLOCK] for b in (1, 2, 0, 3)], axis=1)
    slots = hot(lax.broadcasted_iota(I32, (OWN, ROWS), 0), wanted)

    def outgoing(first):
        moved = dot(slots, lifted[:, first : first + C // 2]).reshape(OWNERS, 8, C // 2)
        blocks = jnp.concatenate([moved[:, :, :LANES], moved[:, :, LANES:]], axis=1).astype(BF16)
        return blocks.reshape(CURVE, TILE, 16, LANES)

    left_one = AlongCurve(left_src, left_mid, sems, 0, curve, tile)
    right_one = AlongTile(right_src, right_mid, sems, 2, curve, tile)
    left_two = AlongTile(left_mid, left_out, sems, 4, curve, tile)
    right_two = AlongCurve(right_mid, right_out, sems, 6, curve, tile)
    left_src[...] = outgoing(0)
    left_one.start()
    left_own = left_one.own(sems.at[8])
    left_own.start()
    right_src[...] = outgoing(C // 2)
    right_one.start()
    right_own = right_one.own(sems.at[9])
    right_own.start()
    left_own.wait()
    left_one.wait_recv()
    left_two.start()
    left_last = left_two.own(sems.at[8])
    left_last.start()
    right_own.wait()
    right_one.wait_recv()
    right_two.start()
    right_last = right_two.own(sems.at[9])
    right_last.start()
    left_last.wait()
    right_last.wait()
    left_two.wait_recv()
    right_two.wait_recv()
    left_one.wait_send()
    right_one.wait_send()
    left_two.wait_send()
    right_two.wait_send()


def conv_call(points, near, slot, gain, weight):
    vmem = pl.BlockSpec(memory_space=pltpu.VMEM)
    half = (CURVE, TILE, 16, LANES)
    return pl.pallas_call(
        conv_kernel,
        out_shape=(jax.ShapeDtypeStruct(half, BF16),) * 2,
        in_specs=[vmem, vmem, vmem, vmem, pl.BlockSpec(memory_space=pl.ANY)],
        out_specs=(vmem, vmem),
        scratch_shapes=[
            pltpu.VMEM((KERNEL * C, C), BF16),
            pltpu.VMEM((ROWS, KERNEL * C), BF16),
            pltpu.VMEM((ROWS + 2 * RIM, C), BF16),
            pltpu.VMEM((ROWS, C), F32),
            pltpu.VMEM(half, BF16),
            pltpu.VMEM(half, BF16),
            pltpu.VMEM(half, BF16),
            pltpu.VMEM(half, BF16),
            pltpu.SemaphoreType.DMA((CHUNKS,)),
            pltpu.SemaphoreType.DMA((14,)),
        ],
        compiler_params=pltpu.CompilerParams(vmem_limit_bytes=VMEM_LIMIT, collective_id=0, has_side_effects=True),
        cost_estimate=pl.CostEstimate(flops=12_000_000_000, bytes_accessed=18_000_000, transcendentals=0),
    )(points, near, slot, gain, weight)


def gelu(v):
    return 0.5 * v * (1.0 + lax.erf(v * (1.0 / math.sqrt(2.0))))


def owner_kernel(
    left_ref, right_ref, from_ref, pick_ref,
    wq_hbm, wk_hbm, wv_hbm, wo_hbm, wu_hbm, wd_hbm, wp_hbm,
    fine_ref, land_ref,
    wq, wk, wv, wo, wu, wd, wp, arranged, query, keys, values, attended, mixed,
    cell_src, cell_mid, cell_turn, weight_sems, sems,
):
    curve, tile = place_of()
    pairs = [(wq_hbm, wq), (wk_hbm, wk), (wv_hbm, wv), (wo_hbm, wo), (wu_hbm, wu), (wd_hbm, wd), (wp_hbm, wp)]
    copies = [pltpu.make_async_copy(src, dst, weight_sems.at[i]) for i, (src, dst) in enumerate(pairs)]
    for copy in copies:
        copy.start()
    barrier = greet(curve, tile)
    tables = jnp.concatenate([from_ref[...], pick_ref[...], jnp.zeros((7, LANES), I32)], axis=0).T
    from_col = jnp.concatenate([tables[:, j : j + 1] for j in range(8)], axis=0)
    pick_col = tables[:, 8:9]
    left = left_ref[...].reshape(OWNERS, 16, LANES).astype(F32)
    right = right_ref[...].reshape(OWNERS, 16, LANES).astype(F32)
    got = jnp.concatenate([left[:, :8], left[:, 8:], right[:, :8], right[:, 8:]], axis=2)
    got = got.astype(BF16).reshape(OWN, C)
    placed = dot(hot(from_col, lax.broadcasted_iota(I32, (OWN, OWN), 1)), got)
    arranged[...] = placed
    normed = norm_rows(placed).astype(BF16)
    live_col = from_col < OWN
    place = lax.broadcasted_iota(I32, (8, LANES), 0) * LANES + lax.broadcasted_iota(I32, (8, LANES), 1)
    first = jnp.min(jnp.where(from_ref[...] < OWN, place, OWN), axis=(0, 1), keepdims=True)
    stand_in = dot(hot(lax.broadcasted_iota(I32, (8, OWN), 1), first), normed)[0:1, :]
    normed_keys = jnp.where(live_col, normed.astype(F32), stand_in).astype(BF16)
    copies[0].wait()
    halves = [wq[:, pl.ds(j * SUB, SUB)] for j in range(C // SUB)]
    wide = dot(normed, jnp.concatenate([x for half in halves for x in (half, half)], axis=1)) * SCALE
    copies[1].wait()
    plain = dot(normed_keys, wk[...])
    copies[2].wait()
    values[...] = dot(normed, wv[...]).astype(BF16)
    most_wide = jnp.maximum(jnp.max(jnp.abs(wide), axis=0, keepdims=True), TINY)
    most_k = jnp.maximum(jnp.max(jnp.abs(plain), axis=0, keepdims=True), TINY)
    most_q = jnp.concatenate([most_wide[:, j * LANES : j * LANES + SUB] for j in range(C // SUB)], axis=1)
    bound = jnp.max(most_q * most_k, axis=1, keepdims=True)
    grow = TOP * lax.rsqrt(bound)
    undo = bound * (1.0 / (TOP * TOP))
    lift = jnp.sqrt(most_k / most_q)
    lift_wide = jnp.concatenate([lift[:, j // 2 * SUB : j // 2 * SUB + SUB] for j in range(2 * C // SUB)], axis=1)
    wide = wide * (lift_wide * grow)
    coarse = wide.astype(F8).astype(F32)
    first_half = lax.rem(lax.broadcasted_iota(I32, (1, 2 * C), 1), LANES) < SUB
    query[...] = jnp.where(first_half, wide, wide - coarse).astype(F8)
    plain = (plain * (grow / lift)).T
    coarse = plain.astype(F8).astype(F32)
    keys[0] = coarse.astype(BF16)
    keys[1] = (plain - coarse).astype(F8).astype(BF16)

    lane = lax.broadcasted_iota(I32, (1, LANES), 1)
    line = lax.broadcasted_iota(I32, (SUB, 1), 0)
    live = jnp.broadcast_to(live_col.astype(F32), (OWN, LANES)).astype(BF16)

    @pl.loop(0, GROUPS)
    def _(g):
        columns = pl.ds(pl.multiple_of(g * LANES, LANES), LANES)
        v_group = values[:, columns]

        @pl.loop(0, OWN // Q_BLOCK)
        def _(b):
            rows = pl.ds(pl.multiple_of(b * Q_BLOCK, Q_BLOCK), Q_BLOCK)
            all_probs, all_values = [], []
            for h in range(PER_GROUP):
                if h % 4 == 0:
                    part = query[rows, pl.ds(pl.multiple_of(g * 2 * LANES + h // 4 * LANES, LANES), LANES)]
                    q_block = jnp.concatenate([part, part], axis=1)
                    lines = pl.ds(pl.multiple_of(g * LANES + h // 4 * SUB, SUB), SUB)
                    k_high, k_low = keys[0, lines, :], keys[1, lines, :]
                first = h % 4 * HEAD
                mine = ((lane >= h * HEAD) & (lane < (h + 1) * HEAD)).astype(F32).astype(BF16)
                mine_lines = ((line >= first) & (line < first + HEAD)).astype(F32).astype(BF16)
                high, low = (k_high * mine_lines).astype(F8), (k_low * mine_lines).astype(F8)
                scores = dot(q_block, jnp.concatenate([high, high, low, low], axis=0))
                top = jnp.max(scores, axis=1, keepdims=True)
                all_probs.append(jnp.exp2((scores - top) * undo).astype(BF16))
                all_values.append(jnp.concatenate([v_group * mine, live * mine], axis=1))
            total = dot(jnp.concatenate(all_probs, axis=1), jnp.concatenate(all_values, axis=0))
            attended[rows, columns] = (total[:, :LANES] / total[:, LANES:]).astype(BF16)

    copies[3].wait()
    mixed[...] = arranged[...] + dot(attended[...], wo[...])
    copies[4].wait()
    copies[5].wait()
    for b in range(OWN // 256):
        rows = pl.ds(b * 256, 256)
        mix = mixed[rows, :]
        second = norm_rows(mix).astype(BF16)
        inner = gelu(dot(second, wu[...])).astype(BF16)
        fine = mix + dot(inner, wd[...])
        fine_ref[rows, :] = jnp.where(live_col[b * 256 : (b + 1) * 256], fine, 0.0).astype(BF16)

    slot = lax.broadcasted_iota(I32, (WIN, OWN), 1) // 8
    cell = lax.broadcasted_iota(I32, (WIN, OWN), 0)
    member = hot(slot, cell)
    sums = dot(member, fine_ref[...])
    counts = dot(member, live)[:, 0:1]
    high = sums.astype(BF16)
    low = (sums - high.astype(F32)).astype(BF16)
    copies[6].wait()
    means = ((dot(high, wp[...]) + dot(low, wp[...])) / jnp.maximum(counts, 1.0)).astype(BF16)
    cells = lax.broadcasted_iota(I32, (WIN, WIN), 1)
    cell_src[...] = dot(hot(pick_col, cells), means).astype(BF16).reshape(CURVE, TILE, C)
    one = AlongCurve(cell_src, cell_mid, sems, 0, curve, tile)
    pl.semaphore_wait(barrier, CURVE + TILE - 2)
    one.start()
    own = one.own(sems.at[4])
    own.start()
    own.wait()
    one.wait_recv()
    row = lax.broadcasted_iota(I32, (WIN, 1), 0)
    turned = lax.rem(row, CURVE) * TILE + lax.div(row, CURVE)
    turn = dot(hot(turned, cells), cell_mid[...].reshape(WIN, C)).reshape(TILE, CURVE, C)
    cell_turn[...] = jnp.concatenate([turn[:, :, : C // 2], turn[:, :, C // 2 :]], axis=1).astype(BF16)

    @pl.loop(1, TILE)
    def _(s):
        peer = lax.rem(tile + s, TILE)
        send(cell_turn.at[peer], land_ref.at[tile], sems, 2, (curve, peer))

    own = pltpu.make_async_copy(cell_turn.at[tile], land_ref.at[tile], sems.at[4])
    own.start()
    own.wait()
    drain(land_ref.at[pl.ds(0, TILE - 1)], sems.at[3])
    one.wait_send()
    drain(cell_turn.at[pl.ds(0, TILE - 1)], sems.at[2])


def owner_call(left, right, from_rows, pick, *weights):
    vmem = pl.BlockSpec(memory_space=pltpu.VMEM)
    hbm = pl.BlockSpec(memory_space=pl.ANY)
    return pl.pallas_call(
        owner_kernel,
        out_shape=(jax.ShapeDtypeStruct((OWN, C), BF16), jax.ShapeDtypeStruct((TILE, 16, C // 2), BF16)),
        in_specs=[vmem] * 4 + [hbm] * 7,
        out_specs=(vmem, vmem),
        scratch_shapes=[
            pltpu.VMEM((C, C), BF16),
            pltpu.VMEM((C, C), BF16),
            pltpu.VMEM((C, C), BF16),
            pltpu.VMEM((C, C), BF16),
            pltpu.VMEM((C, HID), BF16),
            pltpu.VMEM((HID, C), BF16),
            pltpu.VMEM((C, C), BF16),
            pltpu.VMEM((OWN, C), F32),
            pltpu.VMEM((OWN, 2 * C), F8),
            pltpu.VMEM((2, C, OWN), BF16),
            pltpu.VMEM((OWN, C), BF16),
            pltpu.VMEM((OWN, C), BF16),
            pltpu.VMEM((OWN, C), F32),
            pltpu.VMEM((CURVE, TILE, C), BF16),
            pltpu.VMEM((CURVE, TILE, C), BF16),
            pltpu.VMEM((TILE, 16, C // 2), BF16),
            pltpu.SemaphoreType.DMA((7,)),
            pltpu.SemaphoreType.DMA((5,)),
        ],
        compiler_params=pltpu.CompilerParams(vmem_limit_bytes=VMEM_LIMIT, collective_id=1, has_side_effects=True),
        cost_estimate=pl.CostEstimate(flops=40_000_000_000, bytes_accessed=10_000_000, transcendentals=40_000_000),
    )(left, right, from_rows, pick, *weights)


def coarse_kernel(fine_ref, land_ref, cell_ref, gain_ref, fine_out, pooled_ref, sem):
    copy = pltpu.make_async_copy(fine_ref, fine_out, sem)
    copy.start()
    cell_col = jnp.concatenate([cell_ref[...], jnp.zeros((7, LANES), I32)], axis=0).T[:, 0:1]
    cells = lax.broadcasted_iota(I32, (WIN, WIN), 1)
    landed = land_ref[...].astype(F32)
    landed = jnp.concatenate([landed[:, :CURVE], landed[:, CURVE:]], axis=2).astype(BF16).reshape(WIN, C)
    source = lax.rem(cells, CURVE) * TILE + lax.div(cells, CURVE)
    gathered = dot(hot(cell_col, source), landed)
    pooled_ref[...] = gelu(gain_ref[...] * norm_rows(gathered)).astype(BF16)
    copy.wait()


def coarse_call(fine, land, cell_from, gain):
    vmem = pl.BlockSpec(memory_space=pltpu.VMEM)
    hbm = pl.BlockSpec(memory_space=pl.ANY)
    return pl.pallas_call(
        coarse_kernel,
        out_shape=(jax.ShapeDtypeStruct((OWN, C), BF16), jax.ShapeDtypeStruct((WIN, C), BF16)),
        in_specs=[hbm, vmem, vmem, vmem],
        out_specs=(hbm, vmem),
        scratch_shapes=[pltpu.SemaphoreType.DMA(())],
    )(fine, land, cell_from, gain)


AXES = ("curve", "tile")


def shards(
    points, neighbours, conv_weight, cpe_gain, w_query, w_key, w_value, w_out, w_up, w_down, w_pool, pool_gain,
    send_slot, arrival_from, pool_pick, cell_from,
):
    left, right = conv_call(
        points, neighbours, send_slot[None, :], cpe_gain[None, :], conv_weight.reshape(KERNEL * C, C)
    )
    fine, land = owner_call(
        left, right, arrival_from.reshape(8, LANES), pool_pick,
        w_query, w_key, w_value, w_out, w_up, w_down, w_pool,
    )
    return coarse_call(fine, land, cell_from, pool_gain[None, :])


def solution(mesh):
    split = P(AXES)
    rows = P(AXES, None)
    in_specs = (rows, P(None, AXES)) + (P(),) * 10 + (split, split, rows, rows)
    return jax.shard_map(shards, mesh=mesh, in_specs=in_specs, out_specs=(rows, rows), check_vma=False)
```

```python
import math

import jax
import jax.numpy as jnp
from jax import lax
from jax.experimental import pallas as pl
from jax.experimental.pallas import tpu as pltpu
from jax.sharding import PartitionSpec as P

F32 = jnp.float32
BF16 = jnp.bfloat16
I32 = jnp.int32
F8 = jnp.float8_e4m3fn
SUB = 64
TOP = 256.0
TINY = 1e-12

C = 512
HEADS = 32
HEAD = C // HEADS
HID = 2048
KERNEL = 27
OWNERS = 128
OWN = 1024
ROWS = 512
RIM = 64
WIN = 128
BLOCK = 128
CHUNKS = 9
SPAN = KERNEL * C // CHUNKS
CURVE = 8
TILE = 16
MESH = pl.DeviceIdType.MESH
LANES = 128
GROUPS = C // LANES
PER_GROUP = LANES // HEAD
Q_BLOCK = 1024
SCALE = math.log2(math.e) / math.sqrt(HEAD)

VMEM_LIMIT = 60 * 1024 * 1024


def dot(a, b):
    return jnp.dot(a, b, preferred_element_type=F32)


def norm_rows(v):
    centre = jnp.mean(v, axis=-1, keepdims=True)
    shifted = v - centre
    spread = jnp.mean(shifted * shifted, axis=-1, keepdims=True)
    return shifted * lax.rsqrt(spread + 1e-05)


def hot(columns, wanted):
    return (columns == wanted).astype(F32).astype(BF16)


def place_of():
    return lax.axis_index("curve"), lax.axis_index("tile")


def greet(curve, tile):
    barrier = pltpu.get_barrier_semaphore()

    @pl.loop(1, CURVE)
    def _(s):
        pl.semaphore_signal(barrier, inc=1, device_id=(lax.rem(curve + s, CURVE), tile), device_id_type=MESH)

    @pl.loop(1, TILE)
    def _(s):
        pl.semaphore_signal(barrier, inc=1, device_id=(curve, lax.rem(tile + s, TILE)), device_id_type=MESH)

    return barrier


def send(src, dst, sems, i, device):
    pltpu.make_async_remote_copy(
        src_ref=src, dst_ref=dst, send_sem=sems.at[i], recv_sem=sems.at[i + 1], device_id=device, device_id_type=MESH
    ).start()


def drain(ref, sem):
    pltpu.make_async_copy(ref, ref, sem).wait()


class AlongCurve:
    def __init__(self, src, dst, sems, i, curve, tile):
        self.args = src, dst, sems, i, curve, tile

    def start(self):
        src, dst, sems, i, curve, tile = self.args

        @pl.loop(1, CURVE)
        def _(s):
            peer = lax.rem(curve + s, CURVE)
            send(src.at[peer], dst.at[curve], sems, i, (peer, tile))

    def wait_recv(self):
        _, dst, sems, i, _, _ = self.args
        drain(dst.at[pl.ds(0, CURVE - 1)], sems.at[i + 1])

    def wait_send(self):
        src, _, sems, i, _, _ = self.args
        drain(src.at[pl.ds(0, CURVE - 1)], sems.at[i])

    def own(self, sem):
        src, dst, _, _, curve, _ = self.args
        return pltpu.make_async_copy(src.at[curve], dst.at[curve], sem)


class AlongTile:
    def __init__(self, src, dst, sems, i, curve, tile):
        self.args = src, dst, sems, i, curve, tile

    def start(self):
        src, dst, sems, i, curve, tile = self.args

        @pl.loop(1, TILE)
        def _(s):
            peer = lax.rem(tile + s, TILE)
            send(src.at[:, peer], dst.at[:, tile], sems, i, (curve, peer))

    def wait_recv(self):
        _, dst, sems, i, _, _ = self.args
        drain(dst.at[:, pl.ds(0, TILE - 1)], sems.at[i + 1])

    def wait_send(self):
        src, _, sems, i, _, _ = self.args
        drain(src.at[:, pl.ds(0, TILE - 1)], sems.at[i])

    def own(self, sem):
        src, dst, _, _, _, tile = self.args
        return pltpu.make_async_copy(src.at[:, tile], dst.at[:, tile], sem)


def conv_kernel(
    points_ref, near_ref, slot_ref, gain_ref, weight_hbm, left_out, right_out,
    weight, picked, window, total, left_src, right_src, left_mid, right_mid, weight_sems, sems,
):
    curve, tile = place_of()
    me = curve * TILE + tile
    after = lax.rem(me + 1, OWNERS)
    before = lax.rem(me + OWNERS - 1, OWNERS)
    copies = [
        pltpu.make_async_copy(
            weight_hbm.at[pl.ds(c * SPAN, SPAN)], weight.at[pl.ds(c * SPAN, SPAN)], weight_sems.at[c]
        )
        for c in range(CHUNKS)
    ]
    for copy in copies:
        copy.start()
    barrier = greet(curve, tile)
    for peer in (after, before):
        pl.semaphore_signal(
            barrier, inc=1, device_id=(lax.div(peer, TILE), lax.rem(peer, TILE)), device_id_type=MESH
        )
    window[pl.ds(RIM, ROWS), :] = points_ref[...]
    near = near_ref[...] - (ROWS - RIM)
    near = jnp.concatenate([near, jnp.zeros((32 - KERNEL, ROWS), I32)], axis=0).T
    lane = lax.broadcasted_iota(I32, (BLOCK, 2 * BLOCK), 1)

    def pick(b, row):
        local = near[b * BLOCK : (b + 1) * BLOCK] - b * BLOCK
        rows = window[pl.ds(b * BLOCK, 2 * BLOCK), :]
        for k in range(KERNEL):
            picked[pl.ds(row, BLOCK), pl.ds(k * C, C)] = dot(hot(local[:, k : k + 1], lane), rows).astype(BF16)

    def conv(row, count, wait):
        rows = pl.ds(row, count)
        for c in range(CHUNKS):
            if wait:
                copies[c].wait()
            part = dot(picked[rows, pl.ds(c * SPAN, SPAN)], weight[pl.ds(c * SPAN, SPAN), :])
            if c == 0:
                total[rows, :] = part
            else:
                total[rows, :] += part

    pick(1, 0)
    pick(2, BLOCK)
    pl.semaphore_wait(barrier, CURVE + TILE)
    low, high = pl.ds(0, RIM), pl.ds(RIM + ROWS, RIM)
    up = pltpu.make_async_remote_copy(
        src_ref=points_ref.at[pl.ds(ROWS - RIM, RIM)], dst_ref=window.at[low], send_sem=sems.at[10],
        recv_sem=sems.at[11], device_id=(lax.div(after, TILE), lax.rem(after, TILE)), device_id_type=MESH,
    )
    down = pltpu.make_async_remote_copy(
        src_ref=points_ref.at[pl.ds(0, RIM)], dst_ref=window.at[high], send_sem=sems.at[12],
        recv_sem=sems.at[13], device_id=(lax.div(before, TILE), lax.rem(before, TILE)), device_id_type=MESH,
    )
    up.start()
    down.start()
    conv(0, 2 * BLOCK, True)
    up.wait()
    down.wait()

    @pl.when(me == 0)
    def _():
        window[low, :] = jnp.zeros((RIM, C), BF16)

    @pl.when(me == OWNERS - 1)
    def _():
        window[high, :] = jnp.zeros((RIM, C), BF16)

    pick(0, 2 * BLOCK)
    pick(3, 3 * BLOCK)
    conv(2 * BLOCK, 2 * BLOCK, False)
    own = jnp.concatenate([points_ref[pl.ds(b * BLOCK, BLOCK), :] for b in (1, 2, 0, 3)], axis=0)
    lifted = (own.astype(F32) + gain_ref[...] * norm_rows(total[...])).astype(BF16)
    wanted = jnp.concatenate([slot_ref[:, b * BLOCK : (b + 1) * BLOCK] for b in (1, 2, 0, 3)], axis=1)
    slots = hot(lax.broadcasted_iota(I32, (OWN, ROWS), 0), wanted)

    def outgoing(first):
        moved = dot(slots, lifted[:, first : first + C // 2]).reshape(OWNERS, 8, C // 2)
        blocks = jnp.concatenate([moved[:, :, :LANES], moved[:, :, LANES:]], axis=1).astype(BF16)
        return blocks.reshape(CURVE, TILE, 16, LANES)

    left_one = AlongCurve(left_src, left_mid, sems, 0, curve, tile)
    right_one = AlongTile(right_src, right_mid, sems, 2, curve, tile)
    left_two = AlongTile(left_mid, left_out, sems, 4, curve, tile)
    right_two = AlongCurve(right_mid, right_out, sems, 6, curve, tile)
    left_src[...] = outgoing(0)
    left_one.start()
    left_own = left_one.own(sems.at[8])
    left_own.start()
    right_src[...] = outgoing(C // 2)
    right_one.start()
    right_own = right_one.own(sems.at[9])
    right_own.start()
    left_own.wait()
    left_one.wait_recv()
    left_two.start()
    left_last = left_two.own(sems.at[8])
    left_last.start()
    right_own.wait()
    right_one.wait_recv()
    right_two.start()
    right_last = right_two.own(sems.at[9])
    right_last.start()
    left_last.wait()
    right_last.wait()
    left_two.wait_recv()
    right_two.wait_recv()
    left_one.wait_send()
    right_one.wait_send()
    left_two.wait_send()
    right_two.wait_send()


def conv_call(points, near, slot, gain, weight):
    vmem = pl.BlockSpec(memory_space=pltpu.VMEM)
    half = (CURVE, TILE, 16, LANES)
    return pl.pallas_call(
        conv_kernel,
        out_shape=(jax.ShapeDtypeStruct(half, BF16),) * 2,
        in_specs=[vmem, vmem, vmem, vmem, pl.BlockSpec(memory_space=pl.ANY)],
        out_specs=(vmem, vmem),
        scratch_shapes=[
            pltpu.VMEM((KERNEL * C, C), BF16),
            pltpu.VMEM((ROWS, KERNEL * C), BF16),
            pltpu.VMEM((ROWS + 2 * RIM, C), BF16),
            pltpu.VMEM((ROWS, C), F32),
            pltpu.VMEM(half, BF16),
            pltpu.VMEM(half, BF16),
            pltpu.VMEM(half, BF16),
            pltpu.VMEM(half, BF16),
            pltpu.SemaphoreType.DMA((CHUNKS,)),
            pltpu.SemaphoreType.DMA((14,)),
        ],
        compiler_params=pltpu.CompilerParams(vmem_limit_bytes=VMEM_LIMIT, collective_id=0, has_side_effects=True),
        cost_estimate=pl.CostEstimate(flops=12_000_000_000, bytes_accessed=18_000_000, transcendentals=0),
    )(points, near, slot, gain, weight)


def gelu(v):
    return 0.5 * v * (1.0 + lax.erf(v * (1.0 / math.sqrt(2.0))))


def owner_kernel(
    left_ref, right_ref, from_ref, pick_ref,
    wq_hbm, wk_hbm, wv_hbm, wo_hbm, wu_hbm, wd_hbm, wp_hbm,
    fine_ref, land_ref,
    wq, wk, wv, wo, wu, wd, wp, arranged, query, keys, values, attended, mixed,
    cell_src, cell_mid, cell_turn, weight_sems, sems,
):
    curve, tile = place_of()
    pairs = [(wq_hbm, wq), (wk_hbm, wk), (wv_hbm, wv), (wo_hbm, wo), (wu_hbm, wu), (wd_hbm, wd), (wp_hbm, wp)]
    copies = [pltpu.make_async_copy(src, dst, weight_sems.at[i]) for i, (src, dst) in enumerate(pairs)]
    for copy in copies:
        copy.start()
    barrier = greet(curve, tile)
    tables = jnp.concatenate([from_ref[...], pick_ref[...], jnp.zeros((7, LANES), I32)], axis=0).T
    from_col = jnp.concatenate([tables[:, j : j + 1] for j in range(8)], axis=0)
    pick_col = tables[:, 8:9]
    left = left_ref[...].reshape(OWNERS, 16, LANES).astype(F32)
    right = right_ref[...].reshape(OWNERS, 16, LANES).astype(F32)
    got = jnp.concatenate([left[:, :8], left[:, 8:], right[:, :8], right[:, 8:]], axis=2)
    got = got.astype(BF16).reshape(OWN, C)
    placed = dot(hot(from_col, lax.broadcasted_iota(I32, (OWN, OWN), 1)), got)
    arranged[...] = placed
    normed = norm_rows(placed).astype(BF16)
    live_col = from_col < OWN
    place = lax.broadcasted_iota(I32, (8, LANES), 0) * LANES + lax.broadcasted_iota(I32, (8, LANES), 1)
    first = jnp.min(jnp.where(from_ref[...] < OWN, place, OWN), axis=(0, 1), keepdims=True)
    stand_in = dot(hot(lax.broadcasted_iota(I32, (8, OWN), 1), first), normed)[0:1, :]
    normed_keys = jnp.where(live_col, normed.astype(F32), stand_in).astype(BF16)
    copies[0].wait()
    halves = [wq[:, pl.ds(j * SUB, SUB)] for j in range(C // SUB)]
    wide = dot(normed, jnp.concatenate([x for half in halves for x in (half, half)], axis=1)) * SCALE
    copies[1].wait()
    plain = dot(normed_keys, wk[...])
    copies[2].wait()
    values[...] = dot(normed, wv[...]).astype(BF16)
    most_wide = jnp.maximum(jnp.max(jnp.abs(wide), axis=0, keepdims=True), TINY)
    most_k = jnp.maximum(jnp.max(jnp.abs(plain), axis=0, keepdims=True), TINY)
    most_q = jnp.concatenate([most_wide[:, j * LANES : j * LANES + SUB] for j in range(C // SUB)], axis=1)
    bound = jnp.max(most_q * most_k, axis=1, keepdims=True)
    grow = TOP * lax.rsqrt(bound)
    undo = bound * (1.0 / (TOP * TOP))
    lift = jnp.sqrt(most_k / most_q)
    lift_wide = jnp.concatenate([lift[:, j // 2 * SUB : j // 2 * SUB + SUB] for j in range(2 * C // SUB)], axis=1)
    wide = wide * (lift_wide * grow)
    coarse = wide.astype(F8).astype(F32)
    first_half = lax.rem(lax.broadcasted_iota(I32, (1, 2 * C), 1), LANES) < SUB
    query[...] = jnp.where(first_half, wide, wide - coarse).astype(F8)
    plain = (plain * (grow / lift)).T
    coarse = plain.astype(F8).astype(F32)
    keys[0] = coarse.astype(BF16)
    keys[1] = (plain - coarse).astype(F8).astype(BF16)

    lane = lax.broadcasted_iota(I32, (1, LANES), 1)
    line = lax.broadcasted_iota(I32, (SUB, 1), 0)
    live = jnp.broadcast_to(live_col.astype(F32), (OWN, LANES)).astype(BF16)

    @pl.loop(0, GROUPS)
    def _(g):
        columns = pl.ds(pl.multiple_of(g * LANES, LANES), LANES)
        v_group = values[:, columns]

        @pl.loop(0, OWN // Q_BLOCK)
        def _(b):
            rows = pl.ds(pl.multiple_of(b * Q_BLOCK, Q_BLOCK), Q_BLOCK)
            all_probs, all_values = [], []
            for h in range(PER_GROUP):
                if h % 4 == 0:
                    part = query[rows, pl.ds(pl.multiple_of(g * 2 * LANES + h // 4 * LANES, LANES), LANES)]
                    q_block = jnp.concatenate([part, part], axis=1)
                    lines = pl.ds(pl.multiple_of(g * LANES + h // 4 * SUB, SUB), SUB)
                    k_high, k_low = keys[0, lines, :], keys[1, lines, :]
                first = h % 4 * HEAD
                mine = ((lane >= h * HEAD) & (lane < (h + 1) * HEAD)).astype(F32).astype(BF16)
                mine_lines = ((line >= first) & (line < first + HEAD)).astype(F32).astype(BF16)
                high, low = (k_high * mine_lines).astype(F8), (k_low * mine_lines).astype(F8)
                scores = dot(q_block, jnp.concatenate([high, high, low, low], axis=0))
                top = jnp.max(scores, axis=1, keepdims=True)
                all_probs.append(jnp.exp2((scores - top) * undo).astype(BF16))
                all_values.append(jnp.concatenate([v_group * mine, live * mine], axis=1))
            total = dot(jnp.concatenate(all_probs, axis=1), jnp.concatenate(all_values, axis=0))
            attended[rows, columns] = (total[:, :LANES] / total[:, LANES:]).astype(BF16)

    copies[3].wait()
    mixed[...] = arranged[...] + dot(attended[...], wo[...])
    copies[4].wait()
    copies[5].wait()
    for b in range(OWN // 256):
        rows = pl.ds(b * 256, 256)
        mix = mixed[rows, :]
        second = norm_rows(mix).astype(BF16)
        inner = gelu(dot(second, wu[...])).astype(BF16)
        fine = mix + dot(inner, wd[...])
        fine_ref[rows, :] = jnp.where(live_col[b * 256 : (b + 1) * 256], fine, 0.0).astype(BF16)

    slot = lax.broadcasted_iota(I32, (WIN, OWN), 1) // 8
    cell = lax.broadcasted_iota(I32, (WIN, OWN), 0)
    member = hot(slot, cell)
    sums = dot(member, fine_ref[...])
    counts = dot(member, live)[:, 0:1]
    high = sums.astype(BF16)
    low = (sums - high.astype(F32)).astype(BF16)
    copies[6].wait()
    means = ((dot(high, wp[...]) + dot(low, wp[...])) / jnp.maximum(counts, 1.0)).astype(BF16)
    cells = lax.broadcasted_iota(I32, (WIN, WIN), 1)
    cell_src[...] = dot(hot(pick_col, cells), means).astype(BF16).reshape(CURVE, TILE, C)
    one = AlongCurve(cell_src, cell_mid, sems, 0, curve, tile)
    pl.semaphore_wait(barrier, CURVE + TILE - 2)
    one.start()
    own = one.own(sems.at[4])
    own.start()
    own.wait()
    one.wait_recv()
    row = lax.broadcasted_iota(I32, (WIN, 1), 0)
    turned = lax.rem(row, CURVE) * TILE + lax.div(row, CURVE)
    turn = dot(hot(turned, cells), cell_mid[...].reshape(WIN, C)).reshape(TILE, CURVE, C)
    cell_turn[...] = jnp.concatenate([turn[:, :, : C // 2], turn[:, :, C // 2 :]], axis=1).astype(BF16)

    @pl.loop(1, TILE)
    def _(s):
        peer = lax.rem(tile + s, TILE)
        send(cell_turn.at[peer], land_ref.at[tile], sems, 2, (curve, peer))

    own = pltpu.make_async_copy(cell_turn.at[tile], land_ref.at[tile], sems.at[4])
    own.start()
    own.wait()
    drain(land_ref.at[pl.ds(0, TILE - 1)], sems.at[3])
    one.wait_send()
    drain(cell_turn.at[pl.ds(0, TILE - 1)], sems.at[2])


def owner_call(left, right, from_rows, pick, *weights):
    vmem = pl.BlockSpec(memory_space=pltpu.VMEM)
    hbm = pl.BlockSpec(memory_space=pl.ANY)
    return pl.pallas_call(
        owner_kernel,
        out_shape=(jax.ShapeDtypeStruct((OWN, C), BF16), jax.ShapeDtypeStruct((TILE, 16, C // 2), BF16)),
        in_specs=[vmem] * 4 + [hbm] * 7,
        out_specs=(vmem, vmem),
        scratch_shapes=[
            pltpu.VMEM((C, C), BF16),
            pltpu.VMEM((C, C), BF16),
            pltpu.VMEM((C, C), BF16),
            pltpu.VMEM((C, C), BF16),
            pltpu.VMEM((C, HID), BF16),
            pltpu.VMEM((HID, C), BF16),
            pltpu.VMEM((C, C), BF16),
            pltpu.VMEM((OWN, C), F32),
            pltpu.VMEM((OWN, 2 * C), F8),
            pltpu.VMEM((2, C, OWN), BF16),
            pltpu.VMEM((OWN, C), BF16),
            pltpu.VMEM((OWN, C), BF16),
            pltpu.VMEM((OWN, C), F32),
            pltpu.VMEM((CURVE, TILE, C), BF16),
            pltpu.VMEM((CURVE, TILE, C), BF16),
            pltpu.VMEM((TILE, 16, C // 2), BF16),
            pltpu.SemaphoreType.DMA((7,)),
            pltpu.SemaphoreType.DMA((5,)),
        ],
        compiler_params=pltpu.CompilerParams(vmem_limit_bytes=VMEM_LIMIT, collective_id=1, has_side_effects=True),
        cost_estimate=pl.CostEstimate(flops=40_000_000_000, bytes_accessed=10_000_000, transcendentals=40_000_000),
    )(left, right, from_rows, pick, *weights)


def coarse_kernel(fine_ref, land_ref, cell_ref, gain_ref, fine_out, pooled_ref, sem):
    copy = pltpu.make_async_copy(fine_ref, fine_out, sem)
    copy.start()
    cell_col = jnp.concatenate([cell_ref[...], jnp.zeros((7, LANES), I32)], axis=0).T[:, 0:1]
    cells = lax.broadcasted_iota(I32, (WIN, WIN), 1)
    landed = land_ref[...].astype(F32)
    landed = jnp.concatenate([landed[:, :CURVE], landed[:, CURVE:]], axis=2).astype(BF16).reshape(WIN, C)
    source = lax.rem(cells, CURVE) * TILE + lax.div(cells, CURVE)
    gathered = dot(hot(cell_col, source), landed)
    pooled_ref[...] = gelu(gain_ref[...] * norm_rows(gathered)).astype(BF16)
    copy.wait()


def coarse_call(fine, land, cell_from, gain):
    vmem = pl.BlockSpec(memory_space=pltpu.VMEM)
    hbm = pl.BlockSpec(memory_space=pl.ANY)
    return pl.pallas_call(
        coarse_kernel,
        out_shape=(jax.ShapeDtypeStruct((OWN, C), BF16), jax.ShapeDtypeStruct((WIN, C), BF16)),
        in_specs=[vmem] * 4,
        out_specs=(hbm, vmem),
        scratch_shapes=[pltpu.SemaphoreType.DMA(())],
    )(fine, land, cell_from, gain)


AXES = ("curve", "tile")


def shards(
    points, neighbours, conv_weight, cpe_gain, w_query, w_key, w_value, w_out, w_up, w_down, w_pool, pool_gain,
    send_slot, arrival_from, pool_pick, cell_from,
):
    left, right = conv_call(
        points, neighbours, send_slot[None, :], cpe_gain[None, :], conv_weight.reshape(KERNEL * C, C)
    )
    fine, land = owner_call(
        left, right, arrival_from.reshape(8, LANES), pool_pick,
        w_query, w_key, w_value, w_out, w_up, w_down, w_pool,
    )
    return coarse_call(fine, land, cell_from, pool_gain[None, :])


def solution(mesh):
    split = P(AXES)
    rows = P(AXES, None)
    in_specs = (rows, P(None, AXES)) + (P(),) * 10 + (split, split, rows, rows)
    return jax.shard_map(shards, mesh=mesh, in_specs=in_specs, out_specs=(rows, rows), check_vma=False)
```

```python
import math

import jax
import jax.numpy as jnp
from jax import lax
from jax.experimental import pallas as pl
from jax.experimental.pallas import tpu as pltpu
from jax.sharding import PartitionSpec as P

F32 = jnp.float32
BF16 = jnp.bfloat16
I32 = jnp.int32
F8 = jnp.float8_e4m3fn
SUB = 64
TOP = 256.0
TINY = 1e-12

C = 512
HEADS = 32
HEAD = C // HEADS
HID = 2048
KERNEL = 27
OWNERS = 128
OWN = 1024
ROWS = 512
RIM = 64
WIN = 128
BLOCK = 128
CHUNKS = 9
SPAN = KERNEL * C // CHUNKS
CURVE = 8
TILE = 16
MESH = pl.DeviceIdType.MESH
LANES = 128
GROUPS = C // LANES
PER_GROUP = LANES // HEAD
Q_BLOCK = 512
SCALE = math.log2(math.e) / math.sqrt(HEAD)

VMEM_LIMIT = 62 * 1024 * 1024


def dot(a, b):
    return jnp.dot(a, b, preferred_element_type=F32)


def norm_rows(v):
    centre = jnp.mean(v, axis=-1, keepdims=True)
    shifted = v - centre
    spread = jnp.mean(shifted * shifted, axis=-1, keepdims=True)
    return shifted * lax.rsqrt(spread + 1e-05)


def hot(columns, wanted):
    return (columns == wanted).astype(F32).astype(BF16)


def place_of():
    return lax.axis_index("curve"), lax.axis_index("tile")


def greet(curve, tile):
    barrier = pltpu.get_barrier_semaphore()

    @pl.loop(1, CURVE)
    def _(s):
        pl.semaphore_signal(barrier, inc=1, device_id=(lax.rem(curve + s, CURVE), tile), device_id_type=MESH)

    @pl.loop(1, TILE)
    def _(s):
        pl.semaphore_signal(barrier, inc=1, device_id=(curve, lax.rem(tile + s, TILE)), device_id_type=MESH)

    return barrier


def send(src, dst, sems, i, device):
    pltpu.make_async_remote_copy(
        src_ref=src, dst_ref=dst, send_sem=sems.at[i], recv_sem=sems.at[i + 1], device_id=device, device_id_type=MESH
    ).start()


def drain(ref, sem):
    pltpu.make_async_copy(ref, ref, sem).wait()


class AlongCurve:
    def __init__(self, src, dst, sems, i, curve, tile):
        self.args = src, dst, sems, i, curve, tile

    def start(self):
        src, dst, sems, i, curve, tile = self.args

        @pl.loop(1, CURVE)
        def _(s):
            peer = lax.rem(curve + s, CURVE)
            send(src.at[peer], dst.at[curve], sems, i, (peer, tile))

    def wait_recv(self):
        _, dst, sems, i, _, _ = self.args
        drain(dst.at[pl.ds(0, CURVE - 1)], sems.at[i + 1])

    def wait_send(self):
        src, _, sems, i, _, _ = self.args
        drain(src.at[pl.ds(0, CURVE - 1)], sems.at[i])

    def own(self, sem):
        src, dst, _, _, curve, _ = self.args
        return pltpu.make_async_copy(src.at[curve], dst.at[curve], sem)


class AlongTile:
    def __init__(self, src, dst, sems, i, curve, tile):
        self.args = src, dst, sems, i, curve, tile

    def start(self):
        src, dst, sems, i, curve, tile = self.args

        @pl.loop(1, TILE)
        def _(s):
            peer = lax.rem(tile + s, TILE)
            send(src.at[:, peer], dst.at[:, tile], sems, i, (curve, peer))

    def wait_recv(self):
        _, dst, sems, i, _, _ = self.args
        drain(dst.at[:, pl.ds(0, TILE - 1)], sems.at[i + 1])

    def wait_send(self):
        src, _, sems, i, _, _ = self.args
        drain(src.at[:, pl.ds(0, TILE - 1)], sems.at[i])

    def own(self, sem):
        src, dst, _, _, _, tile = self.args
        return pltpu.make_async_copy(src.at[:, tile], dst.at[:, tile], sem)


def gelu(v):
    return 0.5 * v * (1.0 + lax.erf(v * (1.0 / math.sqrt(2.0))))


def block_kernel(
    points_ref, near_ref, slot_ref, gain_ref, from_ref, pick_ref,
    weight_hbm, wq_hbm, wk_hbm, wv_hbm, wo_hbm, wu_hbm, wd_hbm, wp_hbm,
    fine_ref, land_ref,
    weight, picked, window, total, left_src, right_src, left_mid, right_mid, left_out, right_out,
    arranged, query, keys, mixed, cell_src, cell_mid, cell_turn, weight_sems, late_sems, sems, cell_sems,
):
    curve, tile = place_of()
    me = curve * TILE + tile
    after = lax.rem(me + 1, OWNERS)
    before = lax.rem(me + OWNERS - 1, OWNERS)
    copies = [
        pltpu.make_async_copy(
            weight_hbm.at[pl.ds(c * SPAN, SPAN)], weight.at[pl.ds(c * SPAN, SPAN)], weight_sems.at[c]
        )
        for c in range(CHUNKS)
    ]
    for copy in copies:
        copy.start()
    barrier = greet(curve, tile)
    for peer in (after, before):
        pl.semaphore_signal(
            barrier, inc=1, device_id=(lax.div(peer, TILE), lax.rem(peer, TILE)), device_id_type=MESH
        )
    window[pl.ds(RIM, ROWS), :] = points_ref[...]
    near = near_ref[...] - (ROWS - RIM)
    near = jnp.concatenate([near, jnp.zeros((32 - KERNEL, ROWS), I32)], axis=0).T
    lane = lax.broadcasted_iota(I32, (BLOCK, 2 * BLOCK), 1)

    def pick(b, row):
        local = near[b * BLOCK : (b + 1) * BLOCK] - b * BLOCK
        rows = window[pl.ds(b * BLOCK, 2 * BLOCK), :]
        for k in range(KERNEL):
            picked[pl.ds(row, BLOCK), pl.ds(k * C, C)] = dot(hot(local[:, k : k + 1], lane), rows).astype(BF16)

    def conv(row, wait):
        rows = pl.ds(row, 2 * BLOCK)
        for c in range(CHUNKS):
            if wait:
                copies[c].wait()
            part = dot(picked[:, pl.ds(c * SPAN, SPAN)], weight[pl.ds(c * SPAN, SPAN), :])
            if c == 0:
                total[rows, :] = part
            else:
                total[rows, :] += part

    pick(1, 0)
    pick(2, BLOCK)
    pl.semaphore_wait(barrier, CURVE + TILE)
    low, high = pl.ds(0, RIM), pl.ds(RIM + ROWS, RIM)
    up = pltpu.make_async_remote_copy(
        src_ref=points_ref.at[pl.ds(ROWS - RIM, RIM)], dst_ref=window.at[low], send_sem=sems.at[10],
        recv_sem=sems.at[11], device_id=(lax.div(after, TILE), lax.rem(after, TILE)), device_id_type=MESH,
    )
    down = pltpu.make_async_remote_copy(
        src_ref=points_ref.at[pl.ds(0, RIM)], dst_ref=window.at[high], send_sem=sems.at[12],
        recv_sem=sems.at[13], device_id=(lax.div(before, TILE), lax.rem(before, TILE)), device_id_type=MESH,
    )
    up.start()
    down.start()
    conv(0, True)
    up.wait()
    down.wait()

    @pl.when(me == 0)
    def _():
        window[low, :] = jnp.zeros((RIM, C), BF16)

    @pl.when(me == OWNERS - 1)
    def _():
        window[high, :] = jnp.zeros((RIM, C), BF16)

    pick(0, 0)
    pick(3, BLOCK)
    conv(2 * BLOCK, False)
    own = jnp.concatenate([points_ref[pl.ds(b * BLOCK, BLOCK), :] for b in (1, 2, 0, 3)], axis=0)
    lifted = (own.astype(F32) + gain_ref[...] * norm_rows(total[...])).astype(BF16)
    wanted = jnp.concatenate([slot_ref[:, b * BLOCK : (b + 1) * BLOCK] for b in (1, 2, 0, 3)], axis=1)
    slots = hot(lax.broadcasted_iota(I32, (OWN, ROWS), 0), wanted)

    def outgoing(first):
        moved = dot(slots, lifted[:, first : first + C // 2]).reshape(OWNERS, 8, C // 2)
        blocks = jnp.concatenate([moved[:, :, :LANES], moved[:, :, LANES:]], axis=1).astype(BF16)
        return blocks.reshape(CURVE, TILE, 16, LANES)

    left_one = AlongCurve(left_src, left_mid, sems, 0, curve, tile)
    right_one = AlongTile(right_src, right_mid, sems, 2, curve, tile)
    left_two = AlongTile(left_mid, left_out, sems, 4, curve, tile)
    right_two = AlongCurve(right_mid, right_out, sems, 6, curve, tile)
    left_src[...] = outgoing(0)
    left_one.start()
    left_own = left_one.own(sems.at[8])
    left_own.start()
    right_src[...] = outgoing(C // 2)
    right_one.start()
    right_own = right_one.own(sems.at[9])
    right_own.start()

    def room(first, count):
        return weight.at[pl.ds(first, count)]

    wq, wk, wv, wo, wp = (room(i * C, C) for i in range(5))
    wd = room(5 * C, HID)
    ups = [room(9 * C + j * C, C) for j in range(HID // C)]
    values, attended = room(13 * C, OWN), room(15 * C, OWN)
    pairs = [(wq_hbm, wq), (wk_hbm, wk), (wv_hbm, wv), (wo_hbm, wo), (wp_hbm, wp), (wd_hbm, wd)]
    pairs += [(wu_hbm.at[:, pl.ds(j * C, C)], ups[j]) for j in range(HID // C)]
    copies = [pltpu.make_async_copy(src, dst, late_sems.at[i]) for i, (src, dst) in enumerate(pairs)]
    for copy in copies:
        copy.start()
    tables = jnp.concatenate([from_ref[...], pick_ref[...], jnp.zeros((7, LANES), I32)], axis=0).T
    from_col = jnp.concatenate([tables[:, j : j + 1] for j in range(8)], axis=0)
    pick_col = tables[:, 8:9]
    source = lax.broadcasted_iota(I32, (2 * BLOCK, OWN), 1)
    for j in range(4):
        picked[:, pl.ds(j * OWN, OWN)] = hot(from_col[j * 2 * BLOCK : (j + 1) * 2 * BLOCK], source)
    left_own.wait()
    left_one.wait_recv()
    left_two.start()
    left_last = left_two.own(sems.at[8])
    left_last.start()
    right_own.wait()
    right_one.wait_recv()
    right_two.start()
    right_last = right_two.own(sems.at[9])
    right_last.start()
    left_last.wait()
    right_last.wait()
    left_two.wait_recv()
    right_two.wait_recv()
    left_one.wait_send()
    right_one.wait_send()
    left_two.wait_send()
    right_two.wait_send()
    left = left_out[...].reshape(OWNERS, 16, LANES).astype(F32)
    right = right_out[...].reshape(OWNERS, 16, LANES).astype(F32)
    got = jnp.concatenate([left[:, :8], left[:, 8:], right[:, :8], right[:, 8:]], axis=2)
    got = got.astype(BF16).reshape(OWN, C)
    placed = jnp.concatenate([dot(picked[:, pl.ds(j * OWN, OWN)], got) for j in range(4)], axis=0)
    arranged[...] = placed
    normed = norm_rows(placed).astype(BF16)
    live_col = from_col < OWN
    place = lax.broadcasted_iota(I32, (8, LANES), 0) * LANES + lax.broadcasted_iota(I32, (8, LANES), 1)
    first = jnp.min(jnp.where(from_ref[...] < OWN, place, OWN), axis=(0, 1), keepdims=True)
    stand_in = dot(hot(lax.broadcasted_iota(I32, (8, OWN), 1), first), normed)[0:1, :]
    normed_keys = jnp.where(live_col, normed.astype(F32), stand_in).astype(BF16)
    copies[0].wait()
    halves = [wq[:, pl.ds(j * SUB, SUB)] for j in range(C // SUB)]
    wide = dot(normed, jnp.concatenate([x for half in halves for x in (half, half)], axis=1)) * SCALE
    copies[1].wait()
    plain = dot(normed_keys, wk[...])
    copies[2].wait()
    values[...] = dot(normed, wv[...]).astype(BF16)
    most_wide = jnp.maximum(jnp.max(jnp.abs(wide), axis=0, keepdims=True), TINY)
    most_k = jnp.maximum(jnp.max(jnp.abs(plain), axis=0, keepdims=True), TINY)
    most_q = jnp.concatenate([most_wide[:, j * LANES : j * LANES + SUB] for j in range(C // SUB)], axis=1)
    bound = jnp.max(most_q * most_k, axis=1, keepdims=True)
    grow = TOP * lax.rsqrt(bound)
    undo = bound * (1.0 / (TOP * TOP))
    lift = jnp.sqrt(most_k / most_q)
    lift_wide = jnp.concatenate([lift[:, j // 2 * SUB : j // 2 * SUB + SUB] for j in range(2 * C // SUB)], axis=1)
    wide = wide * (lift_wide * grow)
    coarse = wide.astype(F8).astype(F32)
    first_half = lax.rem(lax.broadcasted_iota(I32, (1, 2 * C), 1), LANES) < SUB
    query[...] = jnp.where(first_half, wide, wide - coarse).astype(F8)
    plain = (plain * (grow / lift)).T
    coarse = plain.astype(F8).astype(F32)
    keys[0] = coarse.astype(BF16)
    keys[1] = (plain - coarse).astype(F8).astype(BF16)

    lane = lax.broadcasted_iota(I32, (1, LANES), 1)
    line = lax.broadcasted_iota(I32, (SUB, 1), 0)
    live = jnp.broadcast_to(live_col.astype(F32), (OWN, LANES)).astype(BF16)

    @pl.loop(0, GROUPS)
    def _(g):
        columns = pl.ds(pl.multiple_of(g * LANES, LANES), LANES)
        v_group = values[:, columns]

        @pl.loop(0, OWN // Q_BLOCK)
        def _(b):
            rows = pl.ds(pl.multiple_of(b * Q_BLOCK, Q_BLOCK), Q_BLOCK)
            all_probs, all_values = [], []
            for h in range(PER_GROUP):
                if h % 4 == 0:
                    part = query[rows, pl.ds(pl.multiple_of(g * 2 * LANES + h // 4 * LANES, LANES), LANES)]
                    q_block = jnp.concatenate([part, part], axis=1)
                    lines = pl.ds(pl.multiple_of(g * LANES + h // 4 * SUB, SUB), SUB)
                    k_high, k_low = keys[0, lines, :], keys[1, lines, :]
                first = h % 4 * HEAD
                mine = ((lane >= h * HEAD) & (lane < (h + 1) * HEAD)).astype(F32).astype(BF16)
                mine_lines = ((line >= first) & (line < first + HEAD)).astype(F32).astype(BF16)
                high, low = (k_high * mine_lines).astype(F8), (k_low * mine_lines).astype(F8)
                scores = dot(q_block, jnp.concatenate([high, high, low, low], axis=0))
                top = jnp.max(scores, axis=1, keepdims=True)
                all_probs.append(jnp.exp2((scores - top) * undo).astype(BF16))
                all_values.append(jnp.concatenate([v_group * mine, live * mine], axis=1))
            total = dot(jnp.concatenate(all_probs, axis=1), jnp.concatenate(all_values, axis=0))
            attended[rows, columns] = (total[:, :LANES] / total[:, LANES:]).astype(BF16)

    copies[3].wait()
    mixed[...] = arranged[...] + dot(attended[...], wo[...])
    for copy in copies[5:]:
        copy.wait()
    for b in range(OWN // 256):
        rows = pl.ds(b * 256, 256)
        mix = mixed[rows, :]
        second = norm_rows(mix).astype(BF16)
        inner = jnp.concatenate([gelu(dot(second, up[...])).astype(BF16) for up in ups], axis=1)
        fine = mix + dot(inner, wd[...])
        fine_ref[rows, :] = jnp.where(live_col[b * 256 : (b + 1) * 256], fine, 0.0).astype(BF16)

    slot = lax.broadcasted_iota(I32, (WIN, OWN), 1) // 8
    cell = lax.broadcasted_iota(I32, (WIN, OWN), 0)
    member = hot(slot, cell)
    sums = dot(member, fine_ref[...])
    counts = dot(member, live)[:, 0:1]
    high = sums.astype(BF16)
    low = (sums - high.astype(F32)).astype(BF16)
    copies[4].wait()
    means = ((dot(high, wp[...]) + dot(low, wp[...])) / jnp.maximum(counts, 1.0)).astype(BF16)
    cells = lax.broadcasted_iota(I32, (WIN, WIN), 1)
    cell_src[...] = dot(hot(pick_col, cells), means).astype(BF16).reshape(CURVE, TILE, C)
    one = AlongCurve(cell_src, cell_mid, cell_sems, 0, curve, tile)
    one.start()
    own = one.own(cell_sems.at[4])
    own.start()
    own.wait()
    one.wait_recv()
    row = lax.broadcasted_iota(I32, (WIN, 1), 0)
    turned = lax.rem(row, CURVE) * TILE + lax.div(row, CURVE)
    turn = dot(hot(turned, cells), cell_mid[...].reshape(WIN, C)).reshape(TILE, CURVE, C)
    cell_turn[...] = jnp.concatenate([turn[:, :, : C // 2], turn[:, :, C // 2 :]], axis=1).astype(BF16)

    @pl.loop(1, TILE)
    def _(s):
        peer = lax.rem(tile + s, TILE)
        send(cell_turn.at[peer], land_ref.at[tile], cell_sems, 2, (curve, peer))

    own = pltpu.make_async_copy(cell_turn.at[tile], land_ref.at[tile], cell_sems.at[4])
    own.start()
    own.wait()
    drain(land_ref.at[pl.ds(0, TILE - 1)], cell_sems.at[3])
    one.wait_send()
    drain(cell_turn.at[pl.ds(0, TILE - 1)], cell_sems.at[2])


def block_call(*args):
    vmem = pl.BlockSpec(memory_space=pltpu.VMEM)
    hbm = pl.BlockSpec(memory_space=pl.ANY)
    half = (CURVE, TILE, 16, LANES)
    return pl.pallas_call(
        block_kernel,
        out_shape=(jax.ShapeDtypeStruct((OWN, C), BF16), jax.ShapeDtypeStruct((TILE, 16, C // 2), BF16)),
        in_specs=[vmem] * 6 + [hbm] * 8,
        out_specs=(vmem, vmem),
        scratch_shapes=[
            pltpu.VMEM((KERNEL * C, C), BF16),
            pltpu.VMEM((2 * BLOCK, KERNEL * C), BF16),
            pltpu.VMEM((ROWS + 2 * RIM, C), BF16),
            pltpu.VMEM((ROWS, C), F32),
        ]
        + [pltpu.VMEM(half, BF16)] * 6
        + [
            pltpu.VMEM((OWN, C), F32),
            pltpu.VMEM((OWN, 2 * C), F8),
            pltpu.VMEM((2, C, OWN), BF16),
            pltpu.VMEM((OWN, C), F32),
            pltpu.VMEM((CURVE, TILE, C), BF16),
            pltpu.VMEM((CURVE, TILE, C), BF16),
            pltpu.VMEM((TILE, 16, C // 2), BF16),
            pltpu.SemaphoreType.DMA((CHUNKS,)),
            pltpu.SemaphoreType.DMA((10,)),
            pltpu.SemaphoreType.DMA((14,)),
            pltpu.SemaphoreType.DMA((5,)),
        ],
        compiler_params=pltpu.CompilerParams(vmem_limit_bytes=VMEM_LIMIT, collective_id=0, has_side_effects=True),
        cost_estimate=pl.CostEstimate(flops=50_000_000_000, bytes_accessed=25_000_000, transcendentals=40_000_000),
    )(*args)


def coarse_kernel(fine_ref, land_ref, cell_ref, gain_ref, fine_out, pooled_ref, sem):
    copy = pltpu.make_async_copy(fine_ref, fine_out, sem)
    copy.start()
    cell_col = jnp.concatenate([cell_ref[...], jnp.zeros((7, LANES), I32)], axis=0).T[:, 0:1]
    cells = lax.broadcasted_iota(I32, (WIN, WIN), 1)
    landed = land_ref[...].astype(F32)
    landed = jnp.concatenate([landed[:, :CURVE], landed[:, CURVE:]], axis=2).astype(BF16).reshape(WIN, C)
    source = lax.rem(cells, CURVE) * TILE + lax.div(cells, CURVE)
    gathered = dot(hot(cell_col, source), landed)
    pooled_ref[...] = gelu(gain_ref[...] * norm_rows(gathered)).astype(BF16)
    copy.wait()


def coarse_call(fine, land, cell_from, gain):
    vmem = pl.BlockSpec(memory_space=pltpu.VMEM)
    hbm = pl.BlockSpec(memory_space=pl.ANY)
    return pl.pallas_call(
        coarse_kernel,
        out_shape=(jax.ShapeDtypeStruct((OWN, C), BF16), jax.ShapeDtypeStruct((WIN, C), BF16)),
        in_specs=[vmem] * 4,
        out_specs=(hbm, vmem),
        scratch_shapes=[pltpu.SemaphoreType.DMA(())],
    )(fine, land, cell_from, gain)


AXES = ("curve", "tile")


def shards(
    points, neighbours, conv_weight, cpe_gain, w_query, w_key, w_value, w_out, w_up, w_down, w_pool, pool_gain,
    send_slot, arrival_from, pool_pick, cell_from,
):
    fine, land = block_call(
        points, neighbours, send_slot[None, :], cpe_gain[None, :], arrival_from.reshape(8, LANES), pool_pick,
        conv_weight.reshape(KERNEL * C, C), w_query, w_key, w_value, w_out, w_up, w_down, w_pool,
    )
    return coarse_call(fine, land, cell_from, pool_gain[None, :])


def solution(mesh):
    split = P(AXES)
    rows = P(AXES, None)
    in_specs = (rows, P(None, AXES)) + (P(),) * 10 + (split, split, rows, rows)
    return jax.shard_map(shards, mesh=mesh, in_specs=in_specs, out_specs=(rows, rows), check_vma=False)
```

```python
import math

import jax
import jax.numpy as jnp
from jax import lax
from jax.experimental import pallas as pl
from jax.experimental.pallas import tpu as pltpu
from jax.sharding import PartitionSpec as P

F32 = jnp.float32
BF16 = jnp.bfloat16
I32 = jnp.int32
F8 = jnp.float8_e4m3fn
SUB = 64
TOP = 256.0
TINY = 1e-12

C = 512
HEADS = 32
HEAD = C // HEADS
HID = 2048
KERNEL = 27
OWNERS = 128
OWN = 1024
ROWS = 512
RIM = 64
WIN = 128
BLOCK = 128
CHUNKS = 9
SPAN = KERNEL * C // CHUNKS
CURVE = 8
TILE = 16
MESH = pl.DeviceIdType.MESH
LANES = 128
GROUPS = C // LANES
PER_GROUP = LANES // HEAD
Q_BLOCK = 512
PIECES = 4
SCALE = math.log2(math.e) / math.sqrt(HEAD)

VMEM_LIMIT = 62 * 1024 * 1024


def dot(a, b):
    return jnp.dot(a, b, preferred_element_type=F32)


def norm_rows(v):
    centre = jnp.mean(v, axis=-1, keepdims=True)
    shifted = v - centre
    spread = jnp.mean(shifted * shifted, axis=-1, keepdims=True)
    return shifted * lax.rsqrt(spread + 1e-05)


def hot(columns, wanted):
    return (columns == wanted).astype(F32).astype(BF16)


def place_of():
    return lax.axis_index("curve"), lax.axis_index("tile")


def greet(curve, tile):
    barrier = pltpu.get_barrier_semaphore()

    for s in range(1, CURVE):
        pl.semaphore_signal(barrier, inc=1, device_id=(lax.rem(curve + s, CURVE), tile), device_id_type=MESH)
    for s in range(1, TILE):
        pl.semaphore_signal(barrier, inc=1, device_id=(curve, lax.rem(tile + s, TILE)), device_id_type=MESH)

    return barrier


def send(src, dst, sems, i, device):
    pltpu.make_async_remote_copy(
        src_ref=src, dst_ref=dst, send_sem=sems.at[i], recv_sem=sems.at[i + 1], device_id=device, device_id_type=MESH
    ).start()


def drain(ref, sem):
    pltpu.make_async_copy(ref, ref, sem).wait()


class AlongCurve:
    def __init__(self, src, dst, sems, i, curve, tile):
        self.args = src, dst, sems, i, curve, tile

    def start(self):
        src, dst, sems, i, curve, tile = self.args

        @pl.loop(1, CURVE)
        def _(s):
            peer = lax.rem(curve + s, CURVE)
            send(src.at[peer], dst.at[curve], sems, i, (peer, tile))

    def wait_recv(self):
        _, dst, sems, i, _, _ = self.args
        drain(dst.at[pl.ds(0, CURVE - 1)], sems.at[i + 1])

    def wait_send(self):
        src, _, sems, i, _, _ = self.args
        drain(src.at[pl.ds(0, CURVE - 1)], sems.at[i])

    def own(self, sem):
        src, dst, _, _, curve, _ = self.args
        return pltpu.make_async_copy(src.at[curve], dst.at[curve], sem)


class AlongTile:
    def __init__(self, src, dst, sems, i, curve, tile):
        self.args = src, dst, sems, i, curve, tile

    def start(self):
        src, dst, sems, i, curve, tile = self.args

        @pl.loop(1, TILE)
        def _(s):
            peer = lax.rem(tile + s, TILE)
            send(src.at[:, peer], dst.at[:, tile], sems, i, (curve, peer))

    def wait_recv(self):
        _, dst, sems, i, _, _ = self.args
        drain(dst.at[:, pl.ds(0, TILE - 1)], sems.at[i + 1])

    def wait_send(self):
        src, _, sems, i, _, _ = self.args
        drain(src.at[:, pl.ds(0, TILE - 1)], sems.at[i])

    def own(self, sem):
        src, dst, _, _, _, tile = self.args
        return pltpu.make_async_copy(src.at[:, tile], dst.at[:, tile], sem)


def gelu(v):
    return 0.5 * v * (1.0 + lax.erf(v * (1.0 / math.sqrt(2.0))))


def block_kernel(
    points_ref, near_ref, slot_ref, gain_ref, from_ref, pick_ref,
    weight_hbm, wq_hbm, wk_hbm, wv_hbm, wo_hbm, wu_hbm, wd_hbm, wp_hbm,
    fine_ref, land_ref,
    weight, picked, window, total, slots, left_src, right_src, left_mid, right_mid, left_out, right_out,
    arranged, query, keys, mixed, cell_src, cell_mid, cell_turn, weight_sems, late_sems, sems, cell_sems,
):
    curve, tile = place_of()
    me = curve * TILE + tile
    after = lax.rem(me + 1, OWNERS)
    before = lax.rem(me + OWNERS - 1, OWNERS)
    copies = [
        pltpu.make_async_copy(
            weight_hbm.at[pl.ds(c * SPAN, SPAN)], weight.at[pl.ds(c * SPAN, SPAN)], weight_sems.at[c]
        )
        for c in range(CHUNKS)
    ]
    for copy in copies:
        copy.start()
    barrier = greet(curve, tile)
    for peer in (after, before):
        pl.semaphore_signal(
            barrier, inc=1, device_id=(lax.div(peer, TILE), lax.rem(peer, TILE)), device_id_type=MESH
        )
    window[pl.ds(RIM, ROWS), :] = points_ref[...]
    near = near_ref[...] - (ROWS - RIM)
    near = jnp.concatenate([near, jnp.zeros((32 - KERNEL, ROWS), I32)], axis=0).T
    lane = lax.broadcasted_iota(I32, (BLOCK, 2 * BLOCK), 1)

    def pick(b, row):
        local = near[b * BLOCK : (b + 1) * BLOCK] - b * BLOCK
        rows = window[pl.ds(b * BLOCK, 2 * BLOCK), :]
        for k in range(KERNEL):
            picked[pl.ds(row, BLOCK), pl.ds(k * C, C)] = dot(hot(local[:, k : k + 1], lane), rows).astype(BF16)

    def conv(row, wait):
        rows = pl.ds(row, 2 * BLOCK)
        for c in range(CHUNKS):
            if wait:
                copies[c].wait()
            part = dot(picked[:, pl.ds(c * SPAN, SPAN)], weight[pl.ds(c * SPAN, SPAN), :])
            if c == 0:
                total[rows, :] = part
            else:
                total[rows, :] += part

    pick(1, 0)
    pick(2, BLOCK)
    pl.semaphore_wait(barrier, CURVE + TILE)
    low, high = pl.ds(0, RIM), pl.ds(RIM + ROWS, RIM)
    up = pltpu.make_async_remote_copy(
        src_ref=points_ref.at[pl.ds(ROWS - RIM, RIM)], dst_ref=window.at[low], send_sem=sems.at[10],
        recv_sem=sems.at[11], device_id=(lax.div(after, TILE), lax.rem(after, TILE)), device_id_type=MESH,
    )
    down = pltpu.make_async_remote_copy(
        src_ref=points_ref.at[pl.ds(0, RIM)], dst_ref=window.at[high], send_sem=sems.at[12],
        recv_sem=sems.at[13], device_id=(lax.div(before, TILE), lax.rem(before, TILE)), device_id_type=MESH,
    )
    up.start()
    down.start()
    wanted = jnp.concatenate([slot_ref[:, b * BLOCK : (b + 1) * BLOCK] for b in (1, 2, 0, 3)], axis=1)
    slots[...] = hot(lax.broadcasted_iota(I32, (OWN, ROWS), 0), wanted)
    conv(0, True)
    up.wait()
    down.wait()

    @pl.when(me == 0)
    def _():
        window[low, :] = jnp.zeros((RIM, C), BF16)

    @pl.when(me == OWNERS - 1)
    def _():
        window[high, :] = jnp.zeros((RIM, C), BF16)

    pick(0, 0)
    pick(3, BLOCK)
    conv(2 * BLOCK, False)
    own = jnp.concatenate([points_ref[pl.ds(b * BLOCK, BLOCK), :] for b in (1, 2, 0, 3)], axis=0)
    lifted = (own.astype(F32) + gain_ref[...] * norm_rows(total[...])).astype(BF16)

    def outgoing(first):
        moved = dot(slots[...], lifted[:, first : first + C // 2]).reshape(OWNERS, 8, C // 2)
        blocks = jnp.concatenate([moved[:, :, :LANES], moved[:, :, LANES:]], axis=1).astype(BF16)
        return blocks.reshape(CURVE, TILE, 16, LANES)

    left_one = AlongCurve(left_src, left_mid, sems, 0, curve, tile)
    right_one = AlongTile(right_src, right_mid, sems, 2, curve, tile)
    left_two = AlongTile(left_mid, left_out, sems, 4, curve, tile)
    right_two = AlongCurve(right_mid, right_out, sems, 6, curve, tile)
    left_src[...] = outgoing(0)
    left_one.start()
    left_own = left_one.own(sems.at[8])
    left_own.start()
    right_src[...] = outgoing(C // 2)
    right_one.start()
    right_own = right_one.own(sems.at[9])
    right_own.start()

    def room(first, count):
        return weight.at[pl.ds(first, count)]

    wq, wk, wv, wo, wp = (room(i * C, C) for i in range(5))
    wd = room(5 * C, HID)
    ups = [room(9 * C + j * C, C) for j in range(HID // C)]
    values, attended = room(13 * C, OWN), room(15 * C, OWN)
    pairs = [(wq_hbm, wq), (wk_hbm, wk), (wv_hbm, wv), (wo_hbm, wo), (wp_hbm, wp), (wd_hbm, wd)]
    pairs += [(wu_hbm.at[:, pl.ds(j * C, C)], ups[j]) for j in range(HID // C)]
    copies = [pltpu.make_async_copy(src, dst, late_sems.at[i]) for i, (src, dst) in enumerate(pairs)]
    for copy in copies:
        copy.start()
    tables = jnp.concatenate([from_ref[...], pick_ref[...], jnp.zeros((7, LANES), I32)], axis=0).T
    from_col = jnp.concatenate([tables[:, j : j + 1] for j in range(8)], axis=0)
    pick_col = tables[:, 8:9]
    copies[0].wait()
    twice = [room(17 * C, C), room(18 * C, C)]
    for j in range(2):
        parts = [wq[:, pl.ds(j * C // 2 + i * SUB, SUB)] for i in range(C // 2 // SUB)]
        twice[j][...] = jnp.concatenate([x for part in parts for x in (part, part)], axis=1)
    source = lax.broadcasted_iota(I32, (2 * BLOCK, OWN), 1)
    for j in range(4):
        picked[:, pl.ds(j * OWN, OWN)] = hot(from_col[j * 2 * BLOCK : (j + 1) * 2 * BLOCK], source)
    left_own.wait()
    left_one.wait_recv()
    left_two.start()
    left_last = left_two.own(sems.at[8])
    left_last.start()
    right_own.wait()
    right_one.wait_recv()
    right_two.start()
    right_last = right_two.own(sems.at[9])
    right_last.start()
    left_last.wait()
    right_last.wait()
    left_two.wait_recv()
    right_two.wait_recv()
    left_one.wait_send()
    right_one.wait_send()
    left_two.wait_send()
    right_two.wait_send()
    left = left_out[...].reshape(OWNERS, 16, LANES).astype(F32)
    right = right_out[...].reshape(OWNERS, 16, LANES).astype(F32)
    got = jnp.concatenate([left[:, :8], left[:, 8:], right[:, :8], right[:, 8:]], axis=2)
    got = got.astype(BF16).reshape(OWN, C)
    placed = jnp.concatenate([dot(picked[:, pl.ds(j * OWN, OWN)], got) for j in range(4)], axis=0)
    arranged[...] = placed
    normed = norm_rows(placed).astype(BF16)
    live_col = from_col < OWN
    place = lax.broadcasted_iota(I32, (8, LANES), 0) * LANES + lax.broadcasted_iota(I32, (8, LANES), 1)
    first = jnp.min(jnp.where(from_ref[...] < OWN, place, OWN), axis=(0, 1), keepdims=True)
    stand_in = dot(hot(lax.broadcasted_iota(I32, (8, OWN), 1), first), normed)[0:1, :]
    normed_keys = jnp.where(live_col, normed.astype(F32), stand_in).astype(BF16)
    wide = jnp.concatenate([dot(normed, w[...]) for w in twice], axis=1) * SCALE
    copies[1].wait()
    plain = dot(normed_keys, wk[...])
    copies[2].wait()
    values[...] = dot(normed, wv[...]).astype(BF16)
    most_wide = jnp.maximum(jnp.max(jnp.abs(wide), axis=0, keepdims=True), TINY)
    most_k = jnp.maximum(jnp.max(jnp.abs(plain), axis=0, keepdims=True), TINY)
    most_q = jnp.concatenate([most_wide[:, j * LANES : j * LANES + SUB] for j in range(C // SUB)], axis=1)
    bound = jnp.max(most_q * most_k, axis=1, keepdims=True)
    grow = TOP * lax.rsqrt(bound)
    undo = bound * (1.0 / (TOP * TOP))
    lift = jnp.sqrt(most_k / most_q)
    lift_wide = jnp.concatenate([lift[:, j // 2 * SUB : j // 2 * SUB + SUB] for j in range(2 * C // SUB)], axis=1)
    wide = wide * (lift_wide * grow)
    coarse = wide.astype(F8).astype(F32)
    first_half = lax.rem(lax.broadcasted_iota(I32, (1, 2 * C), 1), LANES) < SUB
    query[...] = jnp.where(first_half, wide, wide - coarse).astype(F8)
    plain = (plain * (grow / lift)).T
    coarse = plain.astype(F8).astype(F32)
    keys[0] = coarse.astype(BF16)
    keys[1] = (plain - coarse).astype(F8).astype(BF16)

    lane = lax.broadcasted_iota(I32, (1, LANES), 1)
    line = lax.broadcasted_iota(I32, (SUB, 1), 0)
    live = jnp.broadcast_to(live_col.astype(F32), (OWN, LANES)).astype(BF16)

    @pl.loop(0, GROUPS)
    def _(g):
        columns = pl.ds(pl.multiple_of(g * LANES, LANES), LANES)
        v_group = values[:, columns]

        @pl.loop(0, OWN // Q_BLOCK)
        def _(b):
            rows = pl.ds(pl.multiple_of(b * Q_BLOCK, Q_BLOCK), Q_BLOCK)
            all_probs, all_values = [], []
            for h in range(PER_GROUP):
                if h % 4 == 0:
                    part = query[rows, pl.ds(pl.multiple_of(g * 2 * LANES + h // 4 * LANES, LANES), LANES)]
                    q_block = jnp.concatenate([part, part], axis=1)
                    lines = pl.ds(pl.multiple_of(g * LANES + h // 4 * SUB, SUB), SUB)
                    k_high, k_low = keys[0, lines, :], keys[1, lines, :]
                first = h % 4 * HEAD
                mine = ((lane >= h * HEAD) & (lane < (h + 1) * HEAD)).astype(F32).astype(BF16)
                mine_lines = ((line >= first) & (line < first + HEAD)).astype(F32).astype(BF16)
                high, low = (k_high * mine_lines).astype(F8), (k_low * mine_lines).astype(F8)
                scores = dot(q_block, jnp.concatenate([high, high, low, low], axis=0))
                top = jnp.max(scores, axis=1, keepdims=True)
                all_probs.append(jnp.exp2((scores - top) * undo).astype(BF16))
                all_values.append(jnp.concatenate([v_group * mine, live * mine], axis=1))
            total = dot(jnp.concatenate(all_probs, axis=1), jnp.concatenate(all_values, axis=0))
            attended[rows, columns] = (total[:, :LANES] / total[:, LANES:]).astype(BF16)

    copies[3].wait()
    mixed[...] = arranged[...] + dot(attended[...], wo[...])
    for copy in copies[5:]:
        copy.wait()
    for b in range(OWN // 512):
        rows = pl.ds(b * 512, 512)
        mix = mixed[rows, :]
        second = norm_rows(mix).astype(BF16)
        inner = jnp.concatenate([gelu(dot(second, up[...])).astype(BF16) for up in ups], axis=1)
        fine = mix + dot(inner, wd[...])
        fine_ref[rows, :] = jnp.where(live_col[b * 512 : (b + 1) * 512], fine, 0.0).astype(BF16)

    slot = lax.broadcasted_iota(I32, (WIN, OWN), 1) // 8
    cell = lax.broadcasted_iota(I32, (WIN, OWN), 0)
    member = hot(slot, cell)
    sums = dot(member, fine_ref[...])
    counts = dot(member, live)[:, 0:1]
    high = sums.astype(BF16)
    low = (sums - high.astype(F32)).astype(BF16)
    copies[4].wait()
    means = ((dot(high, wp[...]) + dot(low, wp[...])) / jnp.maximum(counts, 1.0)).astype(BF16)
    cells = lax.broadcasted_iota(I32, (WIN, WIN), 1)
    cell_src[...] = dot(hot(pick_col, cells), means).astype(BF16).reshape(CURVE, TILE, C)
    one = AlongCurve(cell_src, cell_mid, cell_sems, 0, curve, tile)
    one.start()
    own = one.own(cell_sems.at[4])
    own.start()
    own.wait()
    one.wait_recv()
    row = lax.broadcasted_iota(I32, (WIN, 1), 0)
    turned = lax.rem(row, CURVE) * TILE + lax.div(row, CURVE)
    turn = dot(hot(turned, cells), cell_mid[...].reshape(WIN, C)).reshape(TILE, CURVE, C)
    cell_turn[...] = jnp.concatenate([turn[:, :, : C // 2], turn[:, :, C // 2 :]], axis=1).astype(BF16)

    @pl.loop(1, TILE)
    def _(s):
        peer = lax.rem(tile + s, TILE)
        send(cell_turn.at[peer], land_ref.at[tile], cell_sems, 2, (curve, peer))

    own = pltpu.make_async_copy(cell_turn.at[tile], land_ref.at[tile], cell_sems.at[4])
    own.start()
    own.wait()
    drain(land_ref.at[pl.ds(0, TILE - 1)], cell_sems.at[3])
    one.wait_send()
    drain(cell_turn.at[pl.ds(0, TILE - 1)], cell_sems.at[2])


def block_call(*args):
    vmem = pl.BlockSpec(memory_space=pltpu.VMEM)
    hbm = pl.BlockSpec(memory_space=pl.ANY)
    half = (CURVE, TILE, 16, LANES)
    return pl.pallas_call(
        block_kernel,
        out_shape=(jax.ShapeDtypeStruct((OWN, C), BF16), jax.ShapeDtypeStruct((TILE, 16, C // 2), BF16)),
        in_specs=[vmem] * 6 + [hbm] * 8,
        out_specs=(vmem, vmem),
        scratch_shapes=[
            pltpu.VMEM((KERNEL * C, C), BF16),
            pltpu.VMEM((2 * BLOCK, KERNEL * C), BF16),
            pltpu.VMEM((ROWS + 2 * RIM, C), BF16),
            pltpu.VMEM((ROWS, C), F32),
            pltpu.VMEM((OWN, ROWS), BF16),
        ]
        + [pltpu.VMEM(half, BF16)] * 6
        + [
            pltpu.VMEM((OWN, C), F32),
            pltpu.VMEM((OWN, 2 * C), F8),
            pltpu.VMEM((2, C, OWN), BF16),
            pltpu.VMEM((OWN, C), F32),
            pltpu.VMEM((CURVE, TILE, C), BF16),
            pltpu.VMEM((CURVE, TILE, C), BF16),
            pltpu.VMEM((TILE, 16, C // 2), BF16),
            pltpu.SemaphoreType.DMA((CHUNKS,)),
            pltpu.SemaphoreType.DMA((10,)),
            pltpu.SemaphoreType.DMA((14,)),
            pltpu.SemaphoreType.DMA((5,)),
        ],
        compiler_params=pltpu.CompilerParams(vmem_limit_bytes=VMEM_LIMIT, collective_id=0, has_side_effects=True),
        cost_estimate=pl.CostEstimate(flops=50_000_000_000, bytes_accessed=25_000_000, transcendentals=40_000_000),
    )(*args)


def coarse_kernel(fine_ref, land_ref, cell_ref, gain_ref, fine_out, pooled_ref, held, sem):
    pieces = [pl.ds(i * OWN // PIECES, OWN // PIECES) for i in range(PIECES)]
    into = [pltpu.make_async_copy(fine_ref.at[p], held.at[p], sem.at[0, i]) for i, p in enumerate(pieces)]
    out = [pltpu.make_async_copy(held.at[p], fine_out.at[p], sem.at[1, i]) for i, p in enumerate(pieces)]
    for copy in into:
        copy.start()
    cell_col = jnp.concatenate([cell_ref[...], jnp.zeros((7, LANES), I32)], axis=0).T[:, 0:1]
    cells = lax.broadcasted_iota(I32, (WIN, WIN), 1)
    for i in range(PIECES):
        into[i].wait()
        out[i].start()
    landed = land_ref[...].astype(F32)
    landed = jnp.concatenate([landed[:, :CURVE], landed[:, CURVE:]], axis=2).astype(BF16).reshape(WIN, C)
    source = lax.rem(cells, CURVE) * TILE + lax.div(cells, CURVE)
    gathered = dot(hot(cell_col, source), landed)
    pooled_ref[...] = gelu(gain_ref[...] * norm_rows(gathered)).astype(BF16)
    for copy in out:
        copy.wait()


def coarse_call(fine, land, cell_from, gain):
    vmem = pl.BlockSpec(memory_space=pltpu.VMEM)
    hbm = pl.BlockSpec(memory_space=pl.ANY)
    return pl.pallas_call(
        coarse_kernel,
        out_shape=(jax.ShapeDtypeStruct((OWN, C), BF16), jax.ShapeDtypeStruct((WIN, C), BF16)),
        in_specs=[hbm, vmem, vmem, vmem],
        out_specs=(hbm, vmem),
        scratch_shapes=[pltpu.VMEM((OWN, C), BF16), pltpu.SemaphoreType.DMA((2, PIECES))],
    )(fine, land, cell_from, gain)


AXES = ("curve", "tile")


def shards(
    points, neighbours, conv_weight, cpe_gain, w_query, w_key, w_value, w_out, w_up, w_down, w_pool, pool_gain,
    send_slot, arrival_from, pool_pick, cell_from,
):
    fine, land = block_call(
        points, neighbours, send_slot[None, :], cpe_gain[None, :], arrival_from.reshape(8, LANES), pool_pick,
        conv_weight.reshape(KERNEL * C, C), w_query, w_key, w_value, w_out, w_up, w_down, w_pool,
    )
    return coarse_call(fine, land, cell_from, pool_gain[None, :])


def solution(mesh):
    split = P(AXES)
    rows = P(AXES, None)
    in_specs = (rows, P(None, AXES)) + (P(),) * 10 + (split, split, rows, rows)
    return jax.shard_map(shards, mesh=mesh, in_specs=in_specs, out_specs=(rows, rows), check_vma=False)
```

```python
import math

import jax
import jax.numpy as jnp
from jax import lax
from jax.experimental import pallas as pl
from jax.experimental.pallas import tpu as pltpu
from jax.sharding import PartitionSpec as P

F32 = jnp.float32
BF16 = jnp.bfloat16
I32 = jnp.int32
F8 = jnp.float8_e4m3fn
SUB = 64
TOP = 256.0
TINY = 1e-12

C = 512
HEADS = 32
HEAD = C // HEADS
HID = 2048
KERNEL = 27
OWNERS = 128
OWN = 1024
ROWS = 512
RIM = 64
WIN = 128
BLOCK = 128
CHUNKS = 9
SPAN = KERNEL * C // CHUNKS
CURVE = 8
TILE = 16
MESH = pl.DeviceIdType.MESH
LANES = 128
GROUPS = C // LANES
PER_GROUP = LANES // HEAD
Q_BLOCK = 512
SCALE = math.log2(math.e) / math.sqrt(HEAD)

VMEM_LIMIT = 62 * 1024 * 1024


def dot(a, b):
    return jnp.dot(a, b, preferred_element_type=F32)


def norm_rows(v):
    centre = jnp.mean(v, axis=-1, keepdims=True)
    shifted = v - centre
    spread = jnp.mean(shifted * shifted, axis=-1, keepdims=True)
    return shifted * lax.rsqrt(spread + 1e-05)


def hot(columns, wanted):
    return (columns == wanted).astype(F32).astype(BF16)


def place_of():
    return lax.axis_index("curve"), lax.axis_index("tile")


def greet(curve, tile):
    barrier = pltpu.get_barrier_semaphore()

    for s in range(1, CURVE):
        pl.semaphore_signal(barrier, inc=1, device_id=(lax.rem(curve + s, CURVE), tile), device_id_type=MESH)
    for s in range(1, TILE):
        pl.semaphore_signal(barrier, inc=1, device_id=(curve, lax.rem(tile + s, TILE)), device_id_type=MESH)

    return barrier


def send(src, dst, sems, i, device):
    pltpu.make_async_remote_copy(
        src_ref=src, dst_ref=dst, send_sem=sems.at[i], recv_sem=sems.at[i + 1], device_id=device, device_id_type=MESH
    ).start()


def drain(ref, sem):
    pltpu.make_async_copy(ref, ref, sem).wait()


class AlongCurve:
    def __init__(self, src, dst, sems, i, curve, tile):
        self.args = src, dst, sems, i, curve, tile

    def start(self):
        src, dst, sems, i, curve, tile = self.args

        @pl.loop(1, CURVE)
        def _(s):
            peer = lax.rem(curve + s, CURVE)
            send(src.at[peer], dst.at[curve], sems, i, (peer, tile))

    def wait_recv(self):
        _, dst, sems, i, _, _ = self.args
        drain(dst.at[pl.ds(0, CURVE - 1)], sems.at[i + 1])

    def wait_send(self):
        src, _, sems, i, _, _ = self.args
        drain(src.at[pl.ds(0, CURVE - 1)], sems.at[i])

    def own(self, sem):
        src, dst, _, _, curve, _ = self.args
        return pltpu.make_async_copy(src.at[curve], dst.at[curve], sem)


def gelu(v):
    return 0.5 * v * (1.0 + lax.erf(v * (1.0 / math.sqrt(2.0))))


def block_kernel(
    points_ref, near_ref, slot_ref, gain_ref, from_ref, pick_ref,
    weight_hbm, wq_hbm, wk_hbm, wv_hbm, wo_hbm, wu_hbm, wd_hbm, wp_hbm,
    fine_ref, land_ref,
    weight, picked, window, total, slots, left_src, right_src, left_mid, right_mid, left_out, right_out,
    arranged, query, keys, mixed, cell_src, cell_mid, cell_turn, weight_sems, late_sems, sems, cell_sems,
):
    curve, tile = place_of()
    me = curve * TILE + tile
    after = lax.rem(me + 1, OWNERS)
    before = lax.rem(me + OWNERS - 1, OWNERS)
    copies = [
        pltpu.make_async_copy(
            weight_hbm.at[pl.ds(c * SPAN, SPAN)], weight.at[pl.ds(c * SPAN, SPAN)], weight_sems.at[c]
        )
        for c in range(CHUNKS)
    ]
    for copy in copies:
        copy.start()
    barrier = greet(curve, tile)
    for peer in (after, before):
        pl.semaphore_signal(
            barrier, inc=1, device_id=(lax.div(peer, TILE), lax.rem(peer, TILE)), device_id_type=MESH
        )
    window[pl.ds(RIM, ROWS), :] = points_ref[...]
    near = near_ref[...] - (ROWS - RIM)
    near = jnp.concatenate([near, jnp.zeros((32 - KERNEL, ROWS), I32)], axis=0).T
    lane = lax.broadcasted_iota(I32, (BLOCK, 2 * BLOCK), 1)

    def pick(b, row):
        local = near[b * BLOCK : (b + 1) * BLOCK] - b * BLOCK
        rows = window[pl.ds(b * BLOCK, 2 * BLOCK), :]
        for k in range(KERNEL):
            picked[pl.ds(row, BLOCK), pl.ds(k * C, C)] = dot(hot(local[:, k : k + 1], lane), rows).astype(BF16)

    def conv(row, wait):
        rows = pl.ds(row, 2 * BLOCK)
        for c in range(CHUNKS):
            if wait:
                copies[c].wait()
            part = dot(picked[:, pl.ds(c * SPAN, SPAN)], weight[pl.ds(c * SPAN, SPAN), :])
            if c == 0:
                total[rows, :] = part
            else:
                total[rows, :] += part

    pick(1, 0)
    pick(2, BLOCK)
    pl.semaphore_wait(barrier, CURVE + TILE)
    low, high = pl.ds(0, RIM), pl.ds(RIM + ROWS, RIM)
    up = pltpu.make_async_remote_copy(
        src_ref=points_ref.at[pl.ds(ROWS - RIM, RIM)], dst_ref=window.at[low], send_sem=sems.at[10],
        recv_sem=sems.at[11], device_id=(lax.div(after, TILE), lax.rem(after, TILE)), device_id_type=MESH,
    )
    down = pltpu.make_async_remote_copy(
        src_ref=points_ref.at[pl.ds(0, RIM)], dst_ref=window.at[high], send_sem=sems.at[12],
        recv_sem=sems.at[13], device_id=(lax.div(before, TILE), lax.rem(before, TILE)), device_id_type=MESH,
    )
    up.start()
    down.start()
    wanted = jnp.concatenate([slot_ref[:, b * BLOCK : (b + 1) * BLOCK] for b in (1, 2, 0, 3)], axis=1)
    inner, outer = wanted & (LANES - 1), wanted & (OWN - LANES)
    slot = lax.broadcasted_iota(I32, (OWN, ROWS), 0)
    slots[0] = hot(slot, outer + ((inner + (TILE - tile) * 8) & (LANES - 1)))
    slots[1] = hot(slot, inner + ((outer + (CURVE - curve) * LANES) & (OWN - LANES)))
    conv(0, True)
    up.wait()
    down.wait()

    @pl.when(me == 0)
    def _():
        window[low, :] = jnp.zeros((RIM, C), BF16)

    @pl.when(me == OWNERS - 1)
    def _():
        window[high, :] = jnp.zeros((RIM, C), BF16)

    pick(0, 0)
    pick(3, BLOCK)
    conv(2 * BLOCK, False)
    own = jnp.concatenate([points_ref[pl.ds(b * BLOCK, BLOCK), :] for b in (1, 2, 0, 3)], axis=0)
    lifted = (own.astype(F32) + gain_ref[...] * norm_rows(total[...])).astype(BF16)

    def outgoing(side):
        moved = dot(slots[side], lifted[:, side * C // 2 : (side + 1) * C // 2]).reshape(OWNERS, 8, C // 2)
        blocks = jnp.concatenate([moved[:, :, :LANES], moved[:, :, LANES:]], axis=1).astype(BF16)
        return blocks.reshape(CURVE, TILE, 16, LANES)

    half_t, half_c = TILE // 2, CURVE // 2
    left_sems, right_sems = (0, 14), (2, 16)
    left_src[...] = outgoing(0)
    for q in range(2):
        part = pl.ds(q * half_t, half_t)

        @pl.loop(1, CURVE)
        def _(s):
            peer = lax.rem(curve + s, CURVE)
            send(left_src.at[peer, part], left_mid.at[curve, part], sems, left_sems[q], (peer, tile))

    left_own = pltpu.make_async_copy(left_src.at[curve], left_mid.at[curve], sems.at[8])
    left_own.start()
    right_src[...] = outgoing(1)
    for q in range(2):
        part = pl.ds(q * half_c, half_c)

        @pl.loop(1, TILE)
        def _(s):
            peer = lax.rem(tile + s, TILE)
            send(right_src.at[part, peer], right_mid.at[part, tile], sems, right_sems[q], (curve, peer))

    right_own = pltpu.make_async_copy(right_src.at[:, tile], right_mid.at[:, tile], sems.at[9])
    right_own.start()

    def room(first, count):
        return weight.at[pl.ds(first, count)]

    wq, wk, wv, wo, wp = (room(i * C, C) for i in range(5))
    wd = room(5 * C, HID)
    ups = [room(9 * C + j * C, C) for j in range(HID // C)]
    values, attended = room(13 * C, OWN), room(15 * C, OWN)
    pairs = [(wq_hbm, wq), (wk_hbm, wk), (wv_hbm, wv), (wo_hbm, wo), (wp_hbm, wp), (wd_hbm, wd)]
    pairs += [(wu_hbm.at[:, pl.ds(j * C, C)], ups[j]) for j in range(HID // C)]
    copies = [pltpu.make_async_copy(src, dst, late_sems.at[i]) for i, (src, dst) in enumerate(pairs)]
    for copy in copies:
        copy.start()
    tables = jnp.concatenate([from_ref[...], pick_ref[...], jnp.zeros((7, LANES), I32)], axis=0).T
    from_col = jnp.concatenate([tables[:, j : j + 1] for j in range(8)], axis=0)
    pick_col = tables[:, 8:9]
    copies[0].wait()
    twice = [room(17 * C, C), room(18 * C, C)]
    for j in range(2):
        parts = [wq[:, pl.ds(j * C // 2 + i * SUB, SUB)] for i in range(C // 2 // SUB)]
        twice[j][...] = jnp.concatenate([x for part in parts for x in (part, part)], axis=1)
    source = lax.broadcasted_iota(I32, (2 * BLOCK, OWN), 1)
    for j in range(4):
        picked[:, pl.ds(j * OWN, OWN)] = hot(from_col[j * 2 * BLOCK : (j + 1) * 2 * BLOCK], source)
    left_own.wait()
    right_own.wait()
    left_last = pltpu.make_async_copy(left_mid.at[:, 0], left_out.at[:, tile], sems.at[8])
    right_last = pltpu.make_async_copy(right_mid.at[0], right_out.at[curve], sems.at[9])
    for q in range(2):
        drain(left_mid.at[pl.ds(0, CURVE - 1), pl.ds(0, half_t)], sems.at[left_sems[q] + 1])

        @pl.loop(max(q * half_t, 1), (q + 1) * half_t)
        def _(s):
            send(left_mid.at[:, s], left_out.at[:, tile], sems, 4, (curve, lax.rem(tile + s, TILE)))

        if q == 0:
            left_last.start()
        drain(right_mid.at[pl.ds(0, half_c), pl.ds(0, TILE - 1)], sems.at[right_sems[q] + 1])

        @pl.loop(max(q * half_c, 1), (q + 1) * half_c)
        def _(s):
            send(right_mid.at[s], right_out.at[curve], sems, 6, (lax.rem(curve + s, CURVE), tile))

        if q == 0:
            right_last.start()
    left_last.wait()
    right_last.wait()
    drain(left_out.at[:, pl.ds(0, TILE - 1)], sems.at[5])
    drain(right_out.at[pl.ds(0, CURVE - 1)], sems.at[7])
    for q in range(2):
        drain(left_src.at[pl.ds(0, CURVE - 1), pl.ds(0, half_t)], sems.at[left_sems[q]])
        drain(right_src.at[pl.ds(0, half_c), pl.ds(0, TILE - 1)], sems.at[right_sems[q]])
    drain(left_mid.at[:, pl.ds(0, TILE - 1)], sems.at[4])
    drain(right_mid.at[pl.ds(0, CURVE - 1)], sems.at[6])
    left = left_out[...].reshape(OWNERS, 16, LANES).astype(F32)
    right = right_out[...].reshape(OWNERS, 16, LANES).astype(F32)
    got = jnp.concatenate([left[:, :8], left[:, 8:], right[:, :8], right[:, 8:]], axis=2)
    got = got.astype(BF16).reshape(OWN, C)
    placed = jnp.concatenate([dot(picked[:, pl.ds(j * OWN, OWN)], got) for j in range(4)], axis=0)
    arranged[...] = placed
    normed = norm_rows(placed).astype(BF16)
    live_col = from_col < OWN
    place = lax.broadcasted_iota(I32, (8, LANES), 0) * LANES + lax.broadcasted_iota(I32, (8, LANES), 1)
    first = jnp.min(jnp.where(from_ref[...] < OWN, place, OWN), axis=(0, 1), keepdims=True)
    stand_in = dot(hot(lax.broadcasted_iota(I32, (8, OWN), 1), first), normed)[0:1, :]
    normed_keys = jnp.where(live_col, normed.astype(F32), stand_in).astype(BF16)
    wide = jnp.concatenate([dot(normed, w[...]) for w in twice], axis=1) * SCALE
    copies[1].wait()
    plain = dot(normed_keys, wk[...])
    copies[2].wait()
    values[...] = dot(normed, wv[...]).astype(BF16)
    most_wide = jnp.maximum(jnp.max(jnp.abs(wide), axis=0, keepdims=True), TINY)
    most_k = jnp.maximum(jnp.max(jnp.abs(plain), axis=0, keepdims=True), TINY)
    most_q = jnp.concatenate([most_wide[:, j * LANES : j * LANES + SUB] for j in range(C // SUB)], axis=1)
    bound = jnp.max(most_q * most_k, axis=1, keepdims=True)
    grow = TOP * lax.rsqrt(bound)
    undo = bound * (1.0 / (TOP * TOP))
    lift = jnp.sqrt(most_k / most_q)
    lift_wide = jnp.concatenate([lift[:, j // 2 * SUB : j // 2 * SUB + SUB] for j in range(2 * C // SUB)], axis=1)
    wide = wide * (lift_wide * grow)
    coarse = wide.astype(F8).astype(F32)
    first_half = lax.rem(lax.broadcasted_iota(I32, (1, 2 * C), 1), LANES) < SUB
    query[...] = jnp.where(first_half, wide, wide - coarse).astype(F8)
    plain = (plain * (grow / lift)).T
    coarse = plain.astype(F8).astype(F32)
    keys[0] = coarse.astype(BF16)
    keys[1] = (plain - coarse).astype(F8).astype(BF16)

    lane = lax.broadcasted_iota(I32, (1, LANES), 1)
    line = lax.broadcasted_iota(I32, (SUB, 1), 0)
    live = jnp.broadcast_to(live_col.astype(F32), (OWN, LANES)).astype(BF16)

    @pl.loop(0, GROUPS)
    def _(g):
        columns = pl.ds(pl.multiple_of(g * LANES, LANES), LANES)
        v_group = values[:, columns]

        @pl.loop(0, OWN // Q_BLOCK)
        def _(b):
            rows = pl.ds(pl.multiple_of(b * Q_BLOCK, Q_BLOCK), Q_BLOCK)
            all_probs, all_values = [], []
            for h in range(PER_GROUP):
                if h % 4 == 0:
                    part = query[rows, pl.ds(pl.multiple_of(g * 2 * LANES + h // 4 * LANES, LANES), LANES)]
                    q_block = jnp.concatenate([part, part], axis=1)
                    lines = pl.ds(pl.multiple_of(g * LANES + h // 4 * SUB, SUB), SUB)
                    k_high, k_low = keys[0, lines, :], keys[1, lines, :]
                first = h % 4 * HEAD
                mine = ((lane >= h * HEAD) & (lane < (h + 1) * HEAD)).astype(F32).astype(BF16)
                mine_lines = ((line >= first) & (line < first + HEAD)).astype(F32).astype(BF16)
                high, low = (k_high * mine_lines).astype(F8), (k_low * mine_lines).astype(F8)
                scores = dot(q_block, jnp.concatenate([high, high, low, low], axis=0))
                top = jnp.max(scores, axis=1, keepdims=True)
                all_probs.append(jnp.exp2((scores - top) * undo).astype(BF16))
                all_values.append(jnp.concatenate([v_group * mine, live * mine], axis=1))
            total = dot(jnp.concatenate(all_probs, axis=1), jnp.concatenate(all_values, axis=0))
            attended[rows, columns] = (total[:, :LANES] / total[:, LANES:]).astype(BF16)

    copies[3].wait()
    mixed[...] = arranged[...] + dot(attended[...], wo[...])
    for copy in copies[5:]:
        copy.wait()
    for b in range(OWN // 512):
        rows = pl.ds(b * 512, 512)
        mix = mixed[rows, :]
        second = norm_rows(mix).astype(BF16)
        inner = jnp.concatenate([gelu(dot(second, up[...])).astype(BF16) for up in ups], axis=1)
        fine = mix + dot(inner, wd[...])
        fine_ref[rows, :] = jnp.where(live_col[b * 512 : (b + 1) * 512], fine, 0.0).astype(BF16)

    slot = lax.broadcasted_iota(I32, (WIN, OWN), 1) // 8
    cell = lax.broadcasted_iota(I32, (WIN, OWN), 0)
    member = hot(slot, cell)
    sums = dot(member, fine_ref[...])
    counts = dot(member, live)[:, 0:1]
    high = sums.astype(BF16)
    low = (sums - high.astype(F32)).astype(BF16)
    copies[4].wait()
    means = ((dot(high, wp[...]) + dot(low, wp[...])) / jnp.maximum(counts, 1.0)).astype(BF16)
    cells = lax.broadcasted_iota(I32, (WIN, WIN), 1)
    cell_src[...] = dot(hot(pick_col, cells), means).astype(BF16).reshape(CURVE, TILE, C)
    one = AlongCurve(cell_src, cell_mid, cell_sems, 0, curve, tile)
    one.start()
    own = one.own(cell_sems.at[4])
    own.start()
    own.wait()
    one.wait_recv()
    row = lax.broadcasted_iota(I32, (WIN, 1), 0)
    turned = lax.rem(row, CURVE) * TILE + lax.div(row, CURVE)
    turn = dot(hot(turned, cells), cell_mid[...].reshape(WIN, C)).reshape(TILE, CURVE, C)
    cell_turn[...] = jnp.concatenate([turn[:, :, : C // 2], turn[:, :, C // 2 :]], axis=1).astype(BF16)

    @pl.loop(1, TILE)
    def _(s):
        peer = lax.rem(tile + s, TILE)
        send(cell_turn.at[peer], land_ref.at[tile], cell_sems, 2, (curve, peer))

    own = pltpu.make_async_copy(cell_turn.at[tile], land_ref.at[tile], cell_sems.at[4])
    own.start()
    own.wait()
    drain(land_ref.at[pl.ds(0, TILE - 1)], cell_sems.at[3])
    one.wait_send()
    drain(cell_turn.at[pl.ds(0, TILE - 1)], cell_sems.at[2])


def block_call(*args):
    vmem = pl.BlockSpec(memory_space=pltpu.VMEM)
    hbm = pl.BlockSpec(memory_space=pl.ANY)
    half = (CURVE, TILE, 16, LANES)
    return pl.pallas_call(
        block_kernel,
        out_shape=(jax.ShapeDtypeStruct((OWN, C), BF16), jax.ShapeDtypeStruct((TILE, 16, C // 2), BF16)),
        in_specs=[vmem] * 6 + [hbm] * 8,
        out_specs=(vmem, vmem),
        scratch_shapes=[
            pltpu.VMEM((KERNEL * C, C), BF16),
            pltpu.VMEM((2 * BLOCK, KERNEL * C), BF16),
            pltpu.VMEM((ROWS + 2 * RIM, C), BF16),
            pltpu.VMEM((ROWS, C), F32),
            pltpu.VMEM((2, OWN, ROWS), BF16),
        ]
        + [pltpu.VMEM(half, BF16)] * 6
        + [
            pltpu.VMEM((OWN, C), F32),
            pltpu.VMEM((OWN, 2 * C), F8),
            pltpu.VMEM((2, C, OWN), BF16),
            pltpu.VMEM((OWN, C), F32),
            pltpu.VMEM((CURVE, TILE, C), BF16),
            pltpu.VMEM((CURVE, TILE, C), BF16),
            pltpu.VMEM((TILE, 16, C // 2), BF16),
            pltpu.SemaphoreType.DMA((CHUNKS,)),
            pltpu.SemaphoreType.DMA((10,)),
            pltpu.SemaphoreType.DMA((18,)),
            pltpu.SemaphoreType.DMA((5,)),
        ],
        compiler_params=pltpu.CompilerParams(vmem_limit_bytes=VMEM_LIMIT, collective_id=0, has_side_effects=True),
        cost_estimate=pl.CostEstimate(flops=50_000_000_000, bytes_accessed=25_000_000, transcendentals=40_000_000),
    )(*args)


def coarse_kernel(fine_ref, land_ref, cell_ref, gain_ref, fine_out, pooled_ref, sem):
    copy = pltpu.make_async_copy(fine_ref, fine_out, sem)
    copy.start()
    cell_col = jnp.concatenate([cell_ref[...], jnp.zeros((7, LANES), I32)], axis=0).T[:, 0:1]
    cells = lax.broadcasted_iota(I32, (WIN, WIN), 1)
    landed = land_ref[...].astype(F32)
    landed = jnp.concatenate([landed[:, :CURVE], landed[:, CURVE:]], axis=2).astype(BF16).reshape(WIN, C)
    source = lax.rem(cells, CURVE) * TILE + lax.div(cells, CURVE)
    gathered = dot(hot(cell_col, source), landed)
    pooled_ref[...] = gelu(gain_ref[...] * norm_rows(gathered)).astype(BF16)
    copy.wait()


def coarse_call(fine, land, cell_from, gain):
    vmem = pl.BlockSpec(memory_space=pltpu.VMEM)
    hbm = pl.BlockSpec(memory_space=pl.ANY)
    return pl.pallas_call(
        coarse_kernel,
        out_shape=(jax.ShapeDtypeStruct((OWN, C), BF16), jax.ShapeDtypeStruct((WIN, C), BF16)),
        in_specs=[vmem] * 4,
        out_specs=(hbm, vmem),
        scratch_shapes=[pltpu.SemaphoreType.DMA(())],
    )(fine, land, cell_from, gain)


AXES = ("curve", "tile")


def shards(
    points, neighbours, conv_weight, cpe_gain, w_query, w_key, w_value, w_out, w_up, w_down, w_pool, pool_gain,
    send_slot, arrival_from, pool_pick, cell_from,
):
    fine, land = block_call(
        points, neighbours, send_slot[None, :], cpe_gain[None, :], arrival_from.reshape(8, LANES), pool_pick,
        conv_weight.reshape(KERNEL * C, C), w_query, w_key, w_value, w_out, w_up, w_down, w_pool,
    )
    return coarse_call(fine, land, cell_from, pool_gain[None, :])


def solution(mesh):
    split = P(AXES)
    rows = P(AXES, None)
    in_specs = (rows, P(None, AXES)) + (P(),) * 10 + (split, split, rows, rows)
    return jax.shard_map(shards, mesh=mesh, in_specs=in_specs, out_specs=(rows, rows), check_vma=False)
```

```python
import math

import jax
import jax.numpy as jnp
from jax import lax
from jax.experimental import pallas as pl
from jax.experimental.pallas import tpu as pltpu
from jax.sharding import PartitionSpec as P

F32 = jnp.float32
BF16 = jnp.bfloat16
I32 = jnp.int32
F8 = jnp.float8_e4m3fn
SUB = 64
TOP = 256.0
TINY = 1e-12

C = 512
HEADS = 32
HEAD = C // HEADS
HID = 2048
KERNEL = 27
OWNERS = 128
OWN = 1024
ROWS = 512
RIM = 64
WIN = 128
BLOCK = 128
CHUNKS = 9
SPAN = KERNEL * C // CHUNKS
CURVE = 8
TILE = 16
MESH = pl.DeviceIdType.MESH
LANES = 128
GROUPS = C // LANES
PER_GROUP = LANES // HEAD
Q_BLOCK = 512
SCALE = math.log2(math.e) / math.sqrt(HEAD)

VMEM_LIMIT = 62 * 1024 * 1024


def dot(a, b):
    return jnp.dot(a, b, preferred_element_type=F32)


def norm_rows(v):
    centre = jnp.mean(v, axis=-1, keepdims=True)
    shifted = v - centre
    spread = jnp.mean(shifted * shifted, axis=-1, keepdims=True)
    return shifted * lax.rsqrt(spread + 1e-05)


def hot(columns, wanted):
    return (columns == wanted).astype(F32).astype(BF16)


def place_of():
    return lax.axis_index("curve"), lax.axis_index("tile")


def greet(curve, tile):
    barrier = pltpu.get_barrier_semaphore()

    for s in range(1, CURVE):
        pl.semaphore_signal(barrier, inc=1, device_id=(lax.rem(curve + s, CURVE), tile), device_id_type=MESH)
    for s in range(1, TILE):
        pl.semaphore_signal(barrier, inc=1, device_id=(curve, lax.rem(tile + s, TILE)), device_id_type=MESH)

    return barrier


def send(src, dst, sems, i, device):
    pltpu.make_async_remote_copy(
        src_ref=src, dst_ref=dst, send_sem=sems.at[i], recv_sem=sems.at[i + 1], device_id=device, device_id_type=MESH
    ).start()


def drain(ref, sem):
    pltpu.make_async_copy(ref, ref, sem).wait()


class AlongCurve:
    def __init__(self, src, dst, sems, i, curve, tile):
        self.args = src, dst, sems, i, curve, tile

    def start(self):
        src, dst, sems, i, curve, tile = self.args

        @pl.loop(1, CURVE)
        def _(s):
            peer = lax.rem(curve + s, CURVE)
            send(src.at[peer], dst.at[curve], sems, i, (peer, tile))

    def wait_recv(self):
        _, dst, sems, i, _, _ = self.args
        drain(dst.at[pl.ds(0, CURVE - 1)], sems.at[i + 1])

    def wait_send(self):
        src, _, sems, i, _, _ = self.args
        drain(src.at[pl.ds(0, CURVE - 1)], sems.at[i])

    def own(self, sem):
        src, dst, _, _, curve, _ = self.args
        return pltpu.make_async_copy(src.at[curve], dst.at[curve], sem)


class AlongTile:
    def __init__(self, src, dst, sems, i, curve, tile):
        self.args = src, dst, sems, i, curve, tile

    def start(self):
        src, dst, sems, i, curve, tile = self.args

        @pl.loop(1, TILE)
        def _(s):
            peer = lax.rem(tile + s, TILE)
            send(src.at[:, peer], dst.at[:, tile], sems, i, (curve, peer))

    def wait_recv(self):
        _, dst, sems, i, _, _ = self.args
        drain(dst.at[:, pl.ds(0, TILE - 1)], sems.at[i + 1])

    def wait_send(self):
        src, _, sems, i, _, _ = self.args
        drain(src.at[:, pl.ds(0, TILE - 1)], sems.at[i])

    def own(self, sem):
        src, dst, _, _, _, tile = self.args
        return pltpu.make_async_copy(src.at[:, tile], dst.at[:, tile], sem)


def gelu(v):
    return 0.5 * v * (1.0 + lax.erf(v * (1.0 / math.sqrt(2.0))))


def block_kernel(
    points_ref, near_ref, slot_ref, gain_ref, from_ref, pick_ref,
    weight_hbm, wq_hbm, wk_hbm, wv_hbm, wo_hbm, wu_hbm, wd_hbm, wp_hbm,
    fine_ref, land_ref,
    weight, picked, window, total, slots, left_src, right_src, left_mid, right_mid, left_out, right_out,
    arranged, query, keys, mixed, cell_src, cell_mid, cell_turn, weight_sems, late_sems, sems, cell_sems,
):
    curve, tile = place_of()
    me = curve * TILE + tile
    after = lax.rem(me + 1, OWNERS)
    before = lax.rem(me + OWNERS - 1, OWNERS)
    copies = [
        pltpu.make_async_copy(
            weight_hbm.at[pl.ds(c * SPAN, SPAN)], weight.at[pl.ds(c * SPAN, SPAN)], weight_sems.at[c]
        )
        for c in range(CHUNKS)
    ]
    for copy in copies:
        copy.start()
    barrier = greet(curve, tile)
    for peer in (after, before):
        pl.semaphore_signal(
            barrier, inc=1, device_id=(lax.div(peer, TILE), lax.rem(peer, TILE)), device_id_type=MESH
        )
    window[pl.ds(RIM, ROWS), :] = points_ref[...]
    near = near_ref[...] - (ROWS - RIM)
    near = jnp.concatenate([near, jnp.zeros((32 - KERNEL, ROWS), I32)], axis=0).T
    lane = lax.broadcasted_iota(I32, (BLOCK, 2 * BLOCK), 1)

    def pick(b, row):
        local = near[b * BLOCK : (b + 1) * BLOCK] - b * BLOCK
        rows = window[pl.ds(b * BLOCK, 2 * BLOCK), :]
        for k in range(KERNEL):
            picked[pl.ds(row, BLOCK), pl.ds(k * C, C)] = dot(hot(local[:, k : k + 1], lane), rows).astype(BF16)

    def conv(row, wait):
        rows = pl.ds(row, 2 * BLOCK)
        for c in range(CHUNKS):
            if wait:
                copies[c].wait()
            part = dot(picked[:, pl.ds(c * SPAN, SPAN)], weight[pl.ds(c * SPAN, SPAN), :])
            if c == 0:
                total[rows, :] = part
            else:
                total[rows, :] += part

    pick(1, 0)
    pick(2, BLOCK)
    pl.semaphore_wait(barrier, CURVE + TILE)
    low, high = pl.ds(0, RIM), pl.ds(RIM + ROWS, RIM)
    up = pltpu.make_async_remote_copy(
        src_ref=points_ref.at[pl.ds(ROWS - RIM, RIM)], dst_ref=window.at[low], send_sem=sems.at[10],
        recv_sem=sems.at[11], device_id=(lax.div(after, TILE), lax.rem(after, TILE)), device_id_type=MESH,
    )
    down = pltpu.make_async_remote_copy(
        src_ref=points_ref.at[pl.ds(0, RIM)], dst_ref=window.at[high], send_sem=sems.at[12],
        recv_sem=sems.at[13], device_id=(lax.div(before, TILE), lax.rem(before, TILE)), device_id_type=MESH,
    )
    up.start()
    down.start()
    wanted = jnp.concatenate([slot_ref[:, b * BLOCK : (b + 1) * BLOCK] for b in (1, 2, 0, 3)], axis=1)
    slots[...] = hot(lax.broadcasted_iota(I32, (OWN, ROWS), 0), wanted)
    conv(0, True)
    up.wait()
    down.wait()

    @pl.when(me == 0)
    def _():
        window[low, :] = jnp.zeros((RIM, C), BF16)

    @pl.when(me == OWNERS - 1)
    def _():
        window[high, :] = jnp.zeros((RIM, C), BF16)

    pick(0, 0)
    pick(3, BLOCK)
    conv(2 * BLOCK, False)
    own = jnp.concatenate([points_ref[pl.ds(b * BLOCK, BLOCK), :] for b in (1, 2, 0, 3)], axis=0)
    lifted = (own.astype(F32) + gain_ref[...] * norm_rows(total[...])).astype(BF16)

    def outgoing(first):
        moved = dot(slots[...], lifted[:, first : first + C // 2]).reshape(OWNERS, 8, C // 2)
        blocks = jnp.concatenate([moved[:, :, :LANES], moved[:, :, LANES:]], axis=1).astype(BF16)
        return blocks.reshape(CURVE, TILE, 16, LANES)

    left_one = AlongCurve(left_src, left_mid, sems, 0, curve, tile)
    right_one = AlongTile(right_src, right_mid, sems, 2, curve, tile)
    left_two = AlongTile(left_mid, left_out, sems, 4, curve, tile)
    right_two = AlongCurve(right_mid, right_out, sems, 6, curve, tile)
    left_src[...] = outgoing(0)
    left_one.start()
    left_own = left_one.own(sems.at[8])
    left_own.start()
    right_src[...] = outgoing(C // 2)
    right_one.start()
    right_own = right_one.own(sems.at[9])
    right_own.start()

    def room(first, count):
        return weight.at[pl.ds(first, count)]

    wq, wk, wv, wo, wp = (room(i * C, C) for i in range(5))
    wd = room(5 * C, HID)
    ups = [room(9 * C + j * C, C) for j in range(HID // C)]
    values, attended = room(13 * C, OWN), room(15 * C, OWN)
    pairs = [(wq_hbm, wq), (wk_hbm, wk), (wv_hbm, wv), (wo_hbm, wo), (wp_hbm, wp), (wd_hbm, wd)]
    pairs += [(wu_hbm.at[:, pl.ds(j * C, C)], ups[j]) for j in range(HID // C)]
    copies = [pltpu.make_async_copy(src, dst, late_sems.at[i]) for i, (src, dst) in enumerate(pairs)]
    for copy in copies:
        copy.start()
    tables = jnp.concatenate([from_ref[...], pick_ref[...], jnp.zeros((7, LANES), I32)], axis=0).T
    from_col = jnp.concatenate([tables[:, j : j + 1] for j in range(8)], axis=0)
    pick_col = tables[:, 8:9]
    copies[0].wait()
    twice = [room(17 * C, C), room(18 * C, C)]
    for j in range(2):
        parts = [wq[:, pl.ds(j * C // 2 + i * SUB, SUB)] for i in range(C // 2 // SUB)]
        twice[j][...] = jnp.concatenate([x for part in parts for x in (part, part)], axis=1)
    source = lax.broadcasted_iota(I32, (2 * BLOCK, OWN), 1)
    for j in range(4):
        picked[:, pl.ds(j * OWN, OWN)] = hot(from_col[j * 2 * BLOCK : (j + 1) * 2 * BLOCK], source)
    left_own.wait()
    left_one.wait_recv()
    left_two.start()
    left_last = left_two.own(sems.at[8])
    left_last.start()
    right_own.wait()
    right_one.wait_recv()
    right_two.start()
    right_last = right_two.own(sems.at[9])
    right_last.start()
    left_last.wait()
    right_last.wait()
    left_two.wait_recv()
    right_two.wait_recv()
    left_one.wait_send()
    right_one.wait_send()
    left_two.wait_send()
    right_two.wait_send()
    left = left_out[...].reshape(OWNERS, 16, LANES).astype(F32)
    right = right_out[...].reshape(OWNERS, 16, LANES).astype(F32)
    got = jnp.concatenate([left[:, :8], left[:, 8:], right[:, :8], right[:, 8:]], axis=2)
    got = got.astype(BF16).reshape(OWN, C)
    placed = jnp.concatenate([dot(picked[:, pl.ds(j * OWN, OWN)], got) for j in range(4)], axis=0)
    arranged[...] = placed
    normed = norm_rows(placed).astype(BF16)
    live_col = from_col < OWN
    place = lax.broadcasted_iota(I32, (8, LANES), 0) * LANES + lax.broadcasted_iota(I32, (8, LANES), 1)
    first = jnp.min(jnp.where(from_ref[...] < OWN, place, OWN), axis=(0, 1), keepdims=True)
    stand_in = dot(hot(lax.broadcasted_iota(I32, (8, OWN), 1), first), normed)[0:1, :]
    normed_keys = jnp.where(live_col, normed.astype(F32), stand_in).astype(BF16)
    wide = jnp.concatenate([dot(normed, w[...]) for w in twice], axis=1) * SCALE
    copies[1].wait()
    plain = dot(normed_keys, wk[...])
    copies[2].wait()
    values[...] = dot(normed, wv[...]).astype(BF16)
    most_wide = jnp.maximum(jnp.max(jnp.abs(wide), axis=0, keepdims=True), TINY)
    most_k = jnp.maximum(jnp.max(jnp.abs(plain), axis=0, keepdims=True), TINY)
    most_q = jnp.concatenate([most_wide[:, j * LANES : j * LANES + SUB] for j in range(C // SUB)], axis=1)
    bound = jnp.max(most_q * most_k, axis=1, keepdims=True)
    grow = TOP * lax.rsqrt(bound)
    undo = bound * (1.0 / (TOP * TOP))
    lift = jnp.sqrt(most_k / most_q)
    lift_wide = jnp.concatenate([lift[:, j // 2 * SUB : j // 2 * SUB + SUB] for j in range(2 * C // SUB)], axis=1)
    wide = wide * (lift_wide * grow)
    coarse = wide.astype(F8).astype(F32)
    first_half = lax.rem(lax.broadcasted_iota(I32, (1, 2 * C), 1), LANES) < SUB
    query[...] = jnp.where(first_half, wide, wide - coarse).astype(F8)
    plain = (plain * (grow / lift)).T
    coarse = plain.astype(F8).astype(F32)
    keys[0] = coarse.astype(BF16)
    keys[1] = (plain - coarse).astype(F8).astype(BF16)

    lane = lax.broadcasted_iota(I32, (1, LANES), 1)
    line = lax.broadcasted_iota(I32, (SUB, 1), 0)
    live = jnp.broadcast_to(live_col.astype(F32), (OWN, LANES)).astype(BF16)

    @pl.loop(0, GROUPS)
    def _(g):
        columns = pl.ds(pl.multiple_of(g * LANES, LANES), LANES)
        v_group = values[:, columns]

        @pl.loop(0, OWN // Q_BLOCK)
        def _(b):
            rows = pl.ds(pl.multiple_of(b * Q_BLOCK, Q_BLOCK), Q_BLOCK)
            all_probs, all_values = [], []
            for h in range(PER_GROUP):
                if h % 4 == 0:
                    part = query[rows, pl.ds(pl.multiple_of(g * 2 * LANES + h // 4 * LANES, LANES), LANES)]
                    q_block = jnp.concatenate([part, part], axis=1)
                    lines = pl.ds(pl.multiple_of(g * LANES + h // 4 * SUB, SUB), SUB)
                    k_high, k_low = keys[0, lines, :], keys[1, lines, :]
                first = h % 4 * HEAD
                mine = ((lane >= h * HEAD) & (lane < (h + 1) * HEAD)).astype(F32).astype(BF16)
                mine_lines = ((line >= first) & (line < first + HEAD)).astype(F32).astype(BF16)
                high, low = (k_high * mine_lines).astype(F8), (k_low * mine_lines).astype(F8)
                scores = dot(q_block, jnp.concatenate([high, high, low, low], axis=0))
                top = jnp.max(scores, axis=1, keepdims=True)
                all_probs.append(jnp.exp2((scores - top) * undo).astype(BF16))
                all_values.append(jnp.concatenate([v_group * mine, live * mine], axis=1))
            total = dot(jnp.concatenate(all_probs, axis=1), jnp.concatenate(all_values, axis=0))
            attended[rows, columns] = (total[:, :LANES] / total[:, LANES:]).astype(BF16)

    copies[3].wait()
    mixed[...] = arranged[...] + dot(attended[...], wo[...])
    for copy in copies[5:]:
        copy.wait()
    for b in range(OWN // 512):
        rows = pl.ds(b * 512, 512)
        mix = mixed[rows, :]
        second = norm_rows(mix).astype(BF16)
        inner = jnp.concatenate([gelu(dot(second, up[...])).astype(BF16) for up in ups], axis=1)
        fine = mix + dot(inner, wd[...])
        fine_ref[rows, :] = jnp.where(live_col[b * 512 : (b + 1) * 512], fine, 0.0).astype(BF16)

    slot = lax.broadcasted_iota(I32, (WIN, OWN), 1) // 8
    cell = lax.broadcasted_iota(I32, (WIN, OWN), 0)
    member = hot(slot, cell)
    sums = dot(member, fine_ref[...])
    counts = dot(member, live)[:, 0:1]
    high = sums.astype(BF16)
    low = (sums - high.astype(F32)).astype(BF16)
    copies[4].wait()
    means = ((dot(high, wp[...]) + dot(low, wp[...])) / jnp.maximum(counts, 1.0)).astype(BF16)
    cells = lax.broadcasted_iota(I32, (WIN, WIN), 1)
    cell_src[...] = dot(hot(pick_col, cells), means).astype(BF16).reshape(CURVE, TILE, C)
    one = AlongCurve(cell_src, cell_mid, cell_sems, 0, curve, tile)
    one.start()
    own = one.own(cell_sems.at[4])
    own.start()
    own.wait()
    one.wait_recv()
    row = lax.broadcasted_iota(I32, (WIN, 1), 0)
    turned = lax.rem(row, CURVE) * TILE + lax.div(row, CURVE)
    turn = dot(hot(turned, cells), cell_mid[...].reshape(WIN, C)).reshape(TILE, CURVE, C)
    cell_turn[...] = jnp.concatenate([turn[:, :, : C // 2], turn[:, :, C // 2 :]], axis=1).astype(BF16)

    @pl.loop(1, TILE)
    def _(s):
        peer = lax.rem(tile + s, TILE)
        send(cell_turn.at[peer], land_ref.at[tile], cell_sems, 2, (curve, peer))

    own = pltpu.make_async_copy(cell_turn.at[tile], land_ref.at[tile], cell_sems.at[4])
    own.start()
    own.wait()
    drain(land_ref.at[pl.ds(0, TILE - 1)], cell_sems.at[3])
    one.wait_send()
    drain(cell_turn.at[pl.ds(0, TILE - 1)], cell_sems.at[2])


def block_call(*args):
    vmem = pl.BlockSpec(memory_space=pltpu.VMEM)
    hbm = pl.BlockSpec(memory_space=pl.ANY)
    half = (CURVE, TILE, 16, LANES)
    return pl.pallas_call(
        block_kernel,
        out_shape=(jax.ShapeDtypeStruct((OWN, C), BF16), jax.ShapeDtypeStruct((TILE, 16, C // 2), BF16)),
        in_specs=[vmem] * 6 + [hbm] * 8,
        out_specs=(vmem, vmem),
        scratch_shapes=[
            pltpu.VMEM((KERNEL * C, C), BF16),
            pltpu.VMEM((2 * BLOCK, KERNEL * C), BF16),
            pltpu.VMEM((ROWS + 2 * RIM, C), BF16),
            pltpu.VMEM((ROWS, C), F32),
            pltpu.VMEM((OWN, ROWS), BF16),
        ]
        + [pltpu.VMEM(half, BF16)] * 6
        + [
            pltpu.VMEM((OWN, C), F32),
            pltpu.VMEM((OWN, 2 * C), F8),
            pltpu.VMEM((2, C, OWN), BF16),
            pltpu.VMEM((OWN, C), F32),
            pltpu.VMEM((CURVE, TILE, C), BF16),
            pltpu.VMEM((CURVE, TILE, C), BF16),
            pltpu.VMEM((TILE, 16, C // 2), BF16),
            pltpu.SemaphoreType.DMA((CHUNKS,)),
            pltpu.SemaphoreType.DMA((10,)),
            pltpu.SemaphoreType.DMA((14,)),
            pltpu.SemaphoreType.DMA((5,)),
        ],
        compiler_params=pltpu.CompilerParams(vmem_limit_bytes=VMEM_LIMIT, collective_id=0, has_side_effects=True),
        cost_estimate=pl.CostEstimate(flops=50_000_000_000, bytes_accessed=25_000_000, transcendentals=40_000_000),
    )(*args)


def coarse_kernel(fine_ref, land_ref, cell_ref, gain_ref, fine_out, pooled_ref, sem):
    copy = pltpu.make_async_copy(fine_ref, fine_out, sem)
    copy.start()
    cell_col = jnp.concatenate([cell_ref[...], jnp.zeros((7, LANES), I32)], axis=0).T[:, 0:1]
    cells = lax.broadcasted_iota(I32, (WIN, WIN), 1)
    landed = land_ref[...].astype(F32)
    landed = jnp.concatenate([landed[:, :CURVE], landed[:, CURVE:]], axis=2).astype(BF16).reshape(WIN, C)
    source = lax.rem(cells, CURVE) * TILE + lax.div(cells, CURVE)
    gathered = dot(hot(cell_col, source), landed)
    pooled_ref[...] = gelu(gain_ref[...] * norm_rows(gathered)).astype(BF16)
    copy.wait()


def coarse_call(fine, land, cell_from, gain):
    vmem = pl.BlockSpec(memory_space=pltpu.VMEM)
    hbm = pl.BlockSpec(memory_space=pl.ANY)
    return pl.pallas_call(
        coarse_kernel,
        out_shape=(jax.ShapeDtypeStruct((OWN, C), BF16), jax.ShapeDtypeStruct((WIN, C), BF16)),
        in_specs=[vmem] * 4,
        out_specs=(hbm, vmem),
        scratch_shapes=[pltpu.SemaphoreType.DMA(())],
    )(fine, land, cell_from, gain)


AXES = ("curve", "tile")


def shards(
    points, neighbours, conv_weight, cpe_gain, w_query, w_key, w_value, w_out, w_up, w_down, w_pool, pool_gain,
    send_slot, arrival_from, pool_pick, cell_from,
):
    fine, land = block_call(
        points, neighbours, send_slot[None, :], cpe_gain[None, :], arrival_from.reshape(8, LANES), pool_pick,
        conv_weight.reshape(KERNEL * C, C), w_query, w_key, w_value, w_out, w_up, w_down, w_pool,
    )
    return coarse_call(fine, land, cell_from, pool_gain[None, :])


def solution(mesh):
    split = P(AXES)
    rows = P(AXES, None)
    in_specs = (rows, P(None, AXES)) + (P(),) * 10 + (split, split, rows, rows)
    return jax.shard_map(shards, mesh=mesh, in_specs=in_specs, out_specs=(rows, rows), check_vma=False)
```
